32 devices in a mesh: groups: 2 (over x), bfly: 8 (over z, y), rhs: 2 (over core).
Axes of the slice: x: 2, y: 2, z: 4, core: 2. Of those that a mesh axis runs over, the one named last changes fastest.
Arguments:
- right_sides: bfloat16 [262144, 128], P(('groups', 'bfly', 'rhs')), parts along dimension 0, may hold values from -6 to 6
- leaf_basis: bfloat16 [512, 64, 256], P(('bfly', 'rhs')), may hold values from -0.375 to 0.375
- translations: bfloat16 [512, 9, 64, 128], P(('bfly', 'rhs')), may hold values from -0.5 to 0.5
- node_target: int32 [512], P(('bfly', 'rhs')), may hold values from 0 to 511, as said below
- out_basis: bfloat16 [512, 64, 256], P(('bfly', 'rhs')), may hold values from -0.75 to 0.75
Outputs:
- applied: bfloat16 [262144, 128], P(('groups', 'bfly', 'rhs')), parts along dimension 0
The draws below stay inside these ranges and needn't reach their ends.
There are 2 independent parts, one for each index of `groups`. The reference program is written for one: setup_inputs(seed, part) draws one part's arguments, and reference() takes and returns one part's arrays. A program takes and returns all parts, laid end to end along the dimension named above; an argument that names none is the same for every part. Nothing has to cross between parts.
Inputs may be any that keep to these rules, and one draw needn't show every extreme that they name: node_target is a permutation of the 512 boxes, and node_target[b] // 32 equals r // 32, where r is b with its binary digits (as many as the base-2 logarithm of 512) in reverse order.
All inputs are finite; a program needn't handle non-finite values.
Results may differ from the reference program's by a relative error of at most 0.015.
Values may be sent and summed in bfloat16 or wider, within the bound.
No kernel may reach another device: no remote copies, remote signals or barrier semaphores. Data moves between devices by JAX's collectives and lax.ppermute only.
A program may use at most 64 MiB of HBM per device.

```python
import jax
import jax.numpy as jnp

RANK = 64
COLUMNS = 128
LEAF = 256
BOX_DEV = 32
LEVELS = 9
BOXES = 512
POINTS = 131072


def draw_node_target(key, part):
    key = jax.random.fold_in(key, 7)
    node_index = jnp.arange(BOXES, dtype=jnp.int32)
    reversed_index = jnp.zeros_like(node_index)
    for bit_index in range(LEVELS):
        reversed_index = reversed_index + ((node_index >> bit_index & 1) << LEVELS - 1 - bit_index)
    owners = reversed_index // BOX_DEV
    slot_index = reversed_index % BOX_DEV
    scores = jax.random.randint(key, (BOXES // BOX_DEV, BOX_DEV), 0, 1 << 20) * BOX_DEV
    scores = scores + jnp.arange(BOX_DEV, dtype=jnp.int32)[None, :]
    orders = jnp.argsort(scores, axis=1).astype(jnp.int32)
    return (owners * BOX_DEV + orders[owners, slot_index]).astype(jnp.int32)


def shard_levels(rng, dims, split, low, top_value):
    def one(dim, parts):
        steps = jax.random.uniform(jax.random.fold_in(jax.random.fold_in(rng, 6), dim), (parts,), jnp.float32, low / len(split), top_value / len(split))
        return jnp.repeat(jnp.exp(steps), dims[dim] // parts).reshape((-1,) + (1,) * (len(dims) - dim - 1))

    gain = one(*split[0])
    for cut in split[1:]:
        gain = gain * one(*cut)
    return gain


def gaussian(key, dims, spread, bound, pieces=(), kind=jnp.bfloat16):
    values = spread * jax.random.normal(key, dims, jnp.float32)
    if pieces:
        values = values * shard_levels(key, dims, pieces, -0.22, 0.18)
    return jnp.clip(values, -bound, bound).astype(kind)


def setup_inputs(seed: int = 0, part: int = 0) -> dict:
    splits = jax.random.split(jax.random.key(seed), 6)
    part_splits = jax.random.split(jax.random.fold_in(splits[5], part), 6)
    right_sides = gaussian(part_splits[0], (POINTS, COLUMNS), 1.0, 6.0, ((0, 16),))
    leaf_basis = gaussian(splits[1], (BOXES, RANK, LEAF), LEAF ** -0.5, 0.375, ((0, 16),))
    translations = gaussian(splits[2], (BOXES, LEVELS, RANK, 2 * RANK), (2 * RANK) ** -0.5, 0.5, ((0, 16),))
    node_target = draw_node_target(jax.random.fold_in(splits[5], 71), part)
    out_basis = gaussian(splits[4], (BOXES, RANK, LEAF), RANK ** -0.5, 0.75, ((0, 16),))
    return dict(right_sides=right_sides, leaf_basis=leaf_basis, translations=translations, node_target=node_target, out_basis=out_basis)


def combine(current, partner_part, matrices):
    matrices = matrices.astype(jnp.float32)
    own_term = jnp.einsum('bij,bjc->bic', matrices[:, :, :RANK], current.astype(jnp.float32))
    other_term = jnp.einsum('bij,bjc->bic', matrices[:, :, RANK:], partner_part.astype(jnp.float32))
    return (own_term + other_term).astype(jnp.bfloat16)


def reference(right_sides, leaf_basis, translations, node_target, out_basis):
    point_rows = right_sides.reshape(BOXES, LEAF, COLUMNS).astype(jnp.float32)
    coefficients = jnp.einsum('brl,blc->brc', leaf_basis.astype(jnp.float32), point_rows).astype(jnp.bfloat16)
    for level_index in range(LEVELS):
        span = 2 ** level_index
        blocks = coefficients.reshape(BOXES // (2 * span), 2, span, RANK, COLUMNS)
        partner_part = jnp.flip(blocks, 1).reshape(BOXES, RANK, COLUMNS)
        coefficients = combine(coefficients, partner_part, translations[:, level_index])
    placed = jnp.zeros_like(coefficients).at[node_target].set(coefficients)
    applied = jnp.einsum('brl,brc->blc', out_basis.astype(jnp.float32), placed.astype(jnp.float32))
    return applied.astype(jnp.bfloat16).reshape(BOXES * LEAF, COLUMNS)
```

```python
import jax
import jax.numpy as jnp
from jax import lax
from jax.experimental import pallas as pl
from jax.experimental.pallas import tpu as pltpu
from jax.sharding import PartitionSpec as P

AXES = ("bfly", "rhs")
BF16 = jnp.bfloat16
TILE = 16
VMEM_LIMIT = 48 * 2**20


def from_partner(value, axis, distance):
    mask = 2**distance
    pairs = [(source, source ^ mask) for source in range(lax.axis_size(axis))]
    return lax.ppermute(value, axis, pairs)


def combine(current, partner_part, matrices):
    width = current.shape[1]
    own_term = jnp.einsum(
        "bij,bjc->bic", matrices[:, :, :width], current, preferred_element_type=jnp.float32
    )
    other_term = jnp.einsum(
        "bij,bjc->bic", matrices[:, :, width:], partner_part, preferred_element_type=jnp.float32
    )
    return (own_term + other_term).astype(BF16)


def pack_slots(flat_coefficients, slot_key, capacity, slot_total, target_spot):
    box_count = flat_coefficients.shape[0]
    box_iota = jnp.arange(box_count, dtype=jnp.int32)
    earlier = (slot_key[:, None] == slot_key[None, :]) & (box_iota[None, :] < box_iota[:, None])
    order_within = jnp.sum(earlier.astype(jnp.int32), axis=1)
    slot_of_box = slot_key * capacity + order_within
    selector = jnp.arange(slot_total, dtype=jnp.int32)[:, None] == slot_of_box[None, :]
    outgoing = jnp.dot(
        selector.astype(BF16), flat_coefficients, preferred_element_type=jnp.float32
    ).astype(BF16)
    outgoing_spot = jnp.sum(jnp.where(selector, target_spot[None, :] + 1, 0), axis=1) - 1
    return (outgoing, outgoing_spot)


def exchange_every_level(right_sides, leaf_basis, translations, node_target, out_basis):
    box_count = leaf_basis.shape[0]
    rank_width = leaf_basis.shape[1]
    leaf_rows = leaf_basis.shape[2]
    column_count = right_sides.shape[1]
    point_rows = right_sides.reshape(box_count, leaf_rows, column_count)
    coefficients = jnp.einsum(
        "brl,blc->brc", leaf_basis, point_rows, preferred_element_type=jnp.float32
    ).astype(BF16)
    local_levels = box_count.bit_length() - 1
    for level_index in range(local_levels):
        span = 2**level_index
        blocks = coefficients.reshape(box_count // (2 * span), 2, span, rank_width, column_count)
        partner_part = jnp.flip(blocks, 1).reshape(box_count, rank_width, column_count)
        coefficients = combine(coefficients, partner_part, translations[:, level_index])
    device_count = lax.axis_size(AXES)
    device_levels = device_count.bit_length() - 1
    for section_index in range(device_levels):
        partner_part = from_partner(coefficients, AXES, section_index)
        coefficients = combine(
            coefficients, partner_part, translations[:, local_levels + section_index]
        )
    target_device = node_target // box_count
    target_spot = node_target % box_count
    box_iota = jnp.arange(box_count, dtype=jnp.int32)
    flat_coefficients = coefficients.reshape(box_count, rank_width * column_count)
    capacity = max(1, box_count // device_count)
    slot_total = device_count * capacity
    outgoing, outgoing_spot = pack_slots(
        flat_coefficients, target_device, capacity, slot_total, target_spot
    )
    incoming, incoming_spot = (
        lax.all_to_all(outgoing, AXES, split_axis=0, concat_axis=0, tiled=True),
        lax.all_to_all(outgoing_spot, AXES, split_axis=0, concat_axis=0, tiled=True),
    )
    placement_table = (box_iota[:, None] == incoming_spot[None, :]).astype(BF16)
    placed = jnp.dot(placement_table, incoming, preferred_element_type=jnp.float32).astype(BF16)
    placed = placed.reshape(box_count, rank_width, column_count)
    applied = jnp.einsum("brl,brc->blc", out_basis, placed, preferred_element_type=jnp.float32)
    return applied.astype(BF16).reshape(box_count * leaf_rows, column_count)


def low_index(place, i4, i0):
    z0, y, c = place >> 2, place >> 1 & 1, place & 1
    return i4 * 16 + c * 8 + y * 4 + z0 * 2 + i0


def product(matrix, rows):
    return jnp.dot(matrix, rows, preferred_element_type=jnp.float32).astype(BF16)


def half_index():
    return lax.axis_index("bfly") // (lax.axis_size("bfly") // 2)


def pack_kernel(rank, target_ref, trans_ref, early_ref, late_ref, spots, sem, spot_sem):
    mine = half_index()
    copies = []
    for place in range(8):
        for slot in range(4):
            box = low_index(place, slot & 1, slot >> 1)
            for level in range(2):
                rows = pl.ds((slot * 2 + level) * rank, rank)
                copies.append((trans_ref.at[box, 6 + level], early_ref.at[place, rows]))
        for i4 in range(2):
            box = low_index(place, i4, 0)
            rows = pl.ds((8 + i4) * rank, rank)
            copies.append((trans_ref.at[box + mine, 8], early_ref.at[place, rows]))
            rows = pl.ds(i4 * rank, rank)
            copies.append((trans_ref.at[box + 1 - mine, 8], late_ref.at[place, rows]))
    copies = [pltpu.make_async_copy(source, target, sem) for source, target in copies]
    for copy in copies:
        copy.start()
    first = lax.broadcasted_iota(jnp.int32, (TILE, spots.shape[-1]), 0) == 0
    for place in range(8):
        for side, bit in enumerate((mine, 1 - mine)):
            spot = [target_ref[low_index(place, i4, 0) + bit] % 32 for i4 in range(2)]
            tile = jnp.where(first, spot[0], spot[1]).astype(jnp.float32)
            spots[side, place] = tile.astype(BF16)
    tiles = []
    for place in range(8):
        tiles.append((spots.at[0, place], early_ref.at[place, pl.ds(10 * rank, TILE)]))
        tiles.append((spots.at[1, place], late_ref.at[place, pl.ds(2 * rank, TILE)]))
    tiles = [pltpu.make_async_copy(source, target, spot_sem) for source, target in tiles]
    for copy in tiles:
        copy.start()
    for copy in copies + tiles:
        copy.wait()


def local_kernel(levels, rs_ref, leaf_ref, trans_ref, out_ref, rs, leaf, trans, ping, pong, sem, trans_sem):
    boxes = leaf_ref.shape[0]
    step = boxes // 4
    loads = []
    for part in range(4):
        rows = pl.ds(part * step, step)
        loads.append(
            (
                pltpu.make_async_copy(rs_ref.at[rows], rs.at[rows], sem.at[part, 0]),
                pltpu.make_async_copy(leaf_ref.at[rows], leaf.at[rows], sem.at[part, 1]),
            )
        )
    level_loads = [
        pltpu.make_async_copy(trans_ref.at[:, level], trans.at[level], trans_sem.at[level])
        for level in range(levels)
    ]
    for pair in loads:
        for copy in pair:
            copy.start()
    for copy in level_loads:
        copy.start()
    for part in range(4):
        for copy in loads[part]:
            copy.wait()
        for box in range(part * step, (part + 1) * step):
            ping[box] = product(leaf[box], rs[box])
    source, target = ping, pong
    for level in range(levels):
        level_loads[level].wait()
        if level == levels - 1:
            target = out_ref
        for box in range(boxes):
            rows = jnp.concatenate([source[box], source[box ^ (1 << level)]], axis=0)
            target[box] = product(trans[level, box], rows)
        source, target = target, source


def chip_kernel(level, own_ref, other_ref, trans_ref, out_ref, trans, sem):
    load = pltpu.make_async_copy(trans_ref.at[:, level], trans, sem)
    load.start()
    load.wait()
    for place in range(8):
        for slot in range(4):
            box = low_index(place, slot & 1, slot >> 1)
            rows = jnp.concatenate([own_ref[box], other_ref[box]], axis=0)
            out_ref[place, slot] = product(trans[box], rows)


def quad_kernel(rank, box_ref, trans_ref, keep_ref, send_ref, middle):
    for place in range(8):
        for slot in range(4):
            rows = jnp.concatenate([box_ref[place, slot], box_ref[place ^ 2, slot]], axis=0)
            middle[place, slot] = product(trans_ref[place, pl.ds(slot * 2 * rank, rank)], rows)
    mine = half_index()
    for place in range(8):
        for i4 in range(2):
            for out_ref, bit in ((keep_ref, mine), (send_ref, 1 - mine)):
                slot = bit * 2 + i4
                rows = jnp.concatenate([middle[place, slot], middle[place ^ 4, slot]], axis=0)
                start = pl.multiple_of((slot * 2 + 1) * rank, rank)
                out_ref[place, i4] = product(trans_ref[place, pl.ds(start, rank)], rows)


def final_kernel(rank, keep_ref, recv_ref, early_ref, late_ref, basis_ref, out_ref, result, sem):
    copies = []
    for place in range(8):
        spots = [
            ref[place, pl.ds(start, TILE), :].astype(jnp.float32)
            for ref, start in ((early_ref, 10 * rank), (late_ref, 2 * rank))
        ]
        for i4 in range(2):
            own, other = keep_ref[place, i4], recv_ref[place, i4]
            for side, (ref, start, first, second) in enumerate(
                ((early_ref, 8 + i4, own, other), (late_ref, i4, other, own))
            ):
                rows = jnp.concatenate([first, second], axis=0)
                box = product(ref[place, pl.ds(start * rank, rank)], rows)
                spot = jnp.max(spots[side][i4 : i4 + 1]).astype(jnp.int32)
                slot = place * 4 + i4 * 2 + side
                result[slot] = lax.dot_general(
                    basis_ref[spot],
                    box,
                    (((0,), (0,)), ((), ())),
                    preferred_element_type=jnp.float32,
                ).astype(BF16)
                copy = pltpu.make_async_copy(result.at[slot], out_ref.at[spot], sem)
                copy.start()
                copies.append(copy)
    for copy in copies:
        copy.wait()


def call(kernel, out_shapes, in_spaces, out_spaces, scratch, flops, moved):
    return pl.pallas_call(
        kernel,
        out_shape=out_shapes,
        in_specs=[pl.BlockSpec(memory_space=space) for space in in_spaces],
        out_specs=jax.tree.map(lambda space: pl.BlockSpec(memory_space=space), out_spaces),
        scratch_shapes=scratch,
        compiler_params=pltpu.CompilerParams(vmem_limit_bytes=VMEM_LIMIT),
        cost_estimate=pl.CostEstimate(flops=flops, bytes_accessed=moved, transcendentals=0),
    )


def shape(*dims):
    return jax.ShapeDtypeStruct(dims, BF16)


def bind(kernel, *values):
    return lambda *refs: kernel(*values, *refs)


def move_early(right_sides, leaf_basis, translations, node_target, out_basis):
    boxes, rank, leaf_rows = leaf_basis.shape
    columns = right_sides.shape[1]
    local_levels = boxes.bit_length() - 1
    width = 2 * rank
    block = 2 * rank * columns * 2
    any_, vmem, smem, dma = pl.ANY, pltpu.VMEM, pltpu.SMEM, pltpu.SemaphoreType.DMA
    eighths = [list(range(8)), list(range(8, 16))]

    def among_eight(value):
        rows = value.reshape(-1, value.shape[-1])
        out = lax.all_to_all(rows, AXES, 0, 0, axis_index_groups=eighths, tiled=True)
        return out.reshape(value.shape)

    def across(value):
        return lax.ppermute(value, AXES, [(s, s ^ 8) for s in range(16)])

    early, late = call(
        bind(pack_kernel, rank),
        (shape(8, 10 * rank + TILE, width), shape(8, 2 * rank + TILE, width)),
        (smem, any_),
        (any_, any_),
        [vmem((2, 8, TILE, width), BF16), dma, dma],
        0,
        3 * 2**20,
    )(node_target, translations)
    early = among_eight(early)
    late = across(late)
    coefficients = call(
        bind(local_kernel, local_levels),
        shape(boxes, rank, columns),
        (any_, any_, any_),
        vmem,
        [
            vmem((boxes, leaf_rows, columns), BF16),
            vmem((boxes, rank, leaf_rows), BF16),
            vmem((local_levels, boxes, rank, width), BF16),
            vmem((boxes, rank, columns), BF16),
            vmem((boxes, rank, columns), BF16),
            dma((4, 2)),
            dma((local_levels,)),
        ],
        boxes * rank * columns * 2 * (leaf_rows + local_levels * width),
        6 * 2**20,
    )(right_sides.reshape(boxes, leaf_rows, columns), leaf_basis, translations)
    partner = from_partner(coefficients, AXES, 0)
    coefficients = call(
        bind(chip_kernel, local_levels),
        shape(8, 4, rank, columns),
        (vmem, vmem, any_),
        vmem,
        [vmem((boxes, rank, width), BF16), dma],
        boxes * block * width,
        2**21,
    )(coefficients, partner, translations)
    coefficients = among_eight(coefficients)
    keep, send = call(
        bind(quad_kernel, rank),
        (shape(8, 2, rank, columns), shape(8, 2, rank, columns)),
        (vmem, vmem),
        (vmem, vmem),
        [vmem((8, 4, rank, columns), BF16)],
        2 * boxes * block * width,
        2**21,
    )(coefficients, early)
    received = across(send)
    late = among_eight(late)
    applied = call(
        bind(final_kernel, rank),
        shape(boxes, leaf_rows, columns),
        (vmem, vmem, vmem, vmem, vmem),
        any_,
        [vmem((boxes, leaf_rows, columns), BF16), dma],
        3 * boxes * block * width,
        2**22,
    )(keep, received, early, late, out_basis)
    return applied.reshape(boxes * leaf_rows, columns)


def solution(mesh):
    in_specs = (
        P(("groups", "bfly", "rhs"), None),
        P(("bfly", "rhs"), None, None),
        P(("bfly", "rhs"), None, None, None),
        P(("bfly", "rhs")),
        P(("bfly", "rhs"), None, None),
    )
    out_specs = P(("groups", "bfly", "rhs"), None)

    def per_device(right_sides, leaf_basis, translations, node_target, out_basis):
        devices = lax.axis_size(AXES)
        fits = devices == 16 and leaf_basis.shape[0] == 32
        apply = move_early if fits else exchange_every_level
        return apply(right_sides, leaf_basis, translations, node_target, out_basis)

    return jax.shard_map(
        per_device, mesh=mesh, in_specs=in_specs, out_specs=out_specs, check_vma=False
    )
```

```python
import jax
import jax.numpy as jnp
from jax import lax
from jax.experimental import pallas as pl
from jax.experimental.pallas import tpu as pltpu
from jax.sharding import PartitionSpec as P

AXES = ("bfly", "rhs")
BF16 = jnp.bfloat16
TILE = 16
VMEM_LIMIT = 12 * 2**20


def from_partner(value, axis, distance):
    mask = 2**distance
    pairs = [(source, source ^ mask) for source in range(lax.axis_size(axis))]
    return lax.ppermute(value, axis, pairs)


def combine(current, partner_part, matrices):
    width = current.shape[1]
    own_term = jnp.einsum(
        "bij,bjc->bic", matrices[:, :, :width], current, preferred_element_type=jnp.float32
    )
    other_term = jnp.einsum(
        "bij,bjc->bic", matrices[:, :, width:], partner_part, preferred_element_type=jnp.float32
    )
    return (own_term + other_term).astype(BF16)


def pack_slots(flat_coefficients, slot_key, capacity, slot_total, target_spot):
    box_count = flat_coefficients.shape[0]
    box_iota = jnp.arange(box_count, dtype=jnp.int32)
    earlier = (slot_key[:, None] == slot_key[None, :]) & (box_iota[None, :] < box_iota[:, None])
    order_within = jnp.sum(earlier.astype(jnp.int32), axis=1)
    slot_of_box = slot_key * capacity + order_within
    selector = jnp.arange(slot_total, dtype=jnp.int32)[:, None] == slot_of_box[None, :]
    outgoing = jnp.dot(
        selector.astype(BF16), flat_coefficients, preferred_element_type=jnp.float32
    ).astype(BF16)
    outgoing_spot = jnp.sum(jnp.where(selector, target_spot[None, :] + 1, 0), axis=1) - 1
    return (outgoing, outgoing_spot)


def exchange_every_level(right_sides, leaf_basis, translations, node_target, out_basis):
    box_count = leaf_basis.shape[0]
    rank_width = leaf_basis.shape[1]
    leaf_rows = leaf_basis.shape[2]
    column_count = right_sides.shape[1]
    point_rows = right_sides.reshape(box_count, leaf_rows, column_count)
    coefficients = jnp.einsum(
        "brl,blc->brc", leaf_basis, point_rows, preferred_element_type=jnp.float32
    ).astype(BF16)
    local_levels = box_count.bit_length() - 1
    for level_index in range(local_levels):
        span = 2**level_index
        blocks = coefficients.reshape(box_count // (2 * span), 2, span, rank_width, column_count)
        partner_part = jnp.flip(blocks, 1).reshape(box_count, rank_width, column_count)
        coefficients = combine(coefficients, partner_part, translations[:, level_index])
    device_count = lax.axis_size(AXES)
    device_levels = device_count.bit_length() - 1
    for section_index in range(device_levels):
        partner_part = from_partner(coefficients, AXES, section_index)
        coefficients = combine(
            coefficients, partner_part, translations[:, local_levels + section_index]
        )
    target_device = node_target // box_count
    target_spot = node_target % box_count
    box_iota = jnp.arange(box_count, dtype=jnp.int32)
    flat_coefficients = coefficients.reshape(box_count, rank_width * column_count)
    capacity = max(1, box_count // device_count)
    slot_total = device_count * capacity
    outgoing, outgoing_spot = pack_slots(
        flat_coefficients, target_device, capacity, slot_total, target_spot
    )
    incoming, incoming_spot = (
        lax.all_to_all(outgoing, AXES, split_axis=0, concat_axis=0, tiled=True),
        lax.all_to_all(outgoing_spot, AXES, split_axis=0, concat_axis=0, tiled=True),
    )
    placement_table = (box_iota[:, None] == incoming_spot[None, :]).astype(BF16)
    placed = jnp.dot(placement_table, incoming, preferred_element_type=jnp.float32).astype(BF16)
    placed = placed.reshape(box_count, rank_width, column_count)
    applied = jnp.einsum("brl,brc->blc", out_basis, placed, preferred_element_type=jnp.float32)
    return applied.astype(BF16).reshape(box_count * leaf_rows, column_count)


def product(matrix, rows):
    return jnp.dot(matrix, rows, preferred_element_type=jnp.float32).astype(BF16)


def stacked(first, second):
    return jnp.concatenate([first, second], axis=0)


def own_half():
    return lax.axis_index("bfly") // 4


def own_place():
    return lax.axis_index("bfly") % 4


def first_box(place):
    return (place % 2) * 4 + (place // 2) * 2


def pick(tile, start, step, count, index):
    rows = []
    for k in range(count):
        at = start + step * k
        rows.append(jnp.where(index == 0, tile[at : at + 1], tile[at + 1 : at + 2]))
    return rows


def pack_kernel(rank, target_ref, trans_ref, pair_ref, stay_ref, late_ref, target, sem, target_sem):
    half, own = own_half(), own_place()
    target_copy = pltpu.make_async_copy(target_ref, target, target_sem)
    target_copy.start()
    copies = []
    for place in range(4):
        z0, y = place // 2, place % 2
        source = trans_ref.at[:, y, z0, :, pl.ds(6 * rank, 2 * rank)]
        copies.append(pltpu.make_async_copy(source, pair_ref.at[place], sem))
        for ref, bit in ((stay_ref, half), (late_ref, 1 - half)):
            source = trans_ref.at[:, y, z0, bit, pl.ds(8 * rank, rank)]
            slots = ref.at[place ^ own, pl.ds(0, 4 * rank)].reshape(4, rank, ref.shape[-1])
            copies.append(pltpu.make_async_copy(source, slots, sem))
    for copy in copies:
        copy.start()
    target_copy.wait()
    row = lax.broadcasted_iota(jnp.int32, (TILE, stay_ref.shape[-1]), 0)
    for place in range(4):
        for ref, bit in ((stay_ref, half), (late_ref, 1 - half)):
            spots = [target[q * 8 + first_box(place) + bit] % 32 for q in range(4)]
            tile = jnp.where(
                row < 2,
                jnp.where(row == 0, spots[0], spots[1]),
                jnp.where(row == 2, spots[2], spots[3]),
            )
            ref[place ^ own, pl.ds(4 * rank, TILE), :] = tile.astype(jnp.float32).astype(BF16)
    for copy in copies:
        copy.wait()


def local_kernel(
    levels, rs_ref, leaf_ref, trans_ref, out_ref, next_ref, rs, leaf, trans, ping, pong, sem, trans_sem
):
    boxes = leaf_ref.shape[0]
    step = boxes // 4
    loads = []
    for part in range(4):
        rows = pl.ds(part * step, step)
        loads.append(
            (
                pltpu.make_async_copy(rs_ref.at[rows], rs.at[rows], sem.at[part, 0]),
                pltpu.make_async_copy(leaf_ref.at[rows], leaf.at[rows], sem.at[part, 1]),
            )
        )
    level_loads = [
        pltpu.make_async_copy(trans_ref.at[:, level], trans.at[level], trans_sem.at[level])
        for level in range(levels)
    ]
    level_loads.append(
        pltpu.make_async_copy(trans_ref.at[:, levels], next_ref, trans_sem.at[levels])
    )
    for pair in loads:
        for copy in pair:
            copy.start()
    for copy in level_loads:
        copy.start()
    for part in range(4):
        for copy in loads[part]:
            copy.wait()
        for box in range(part * step, (part + 1) * step):
            ping[box] = product(leaf[box], rs[box])
    source, target = ping, pong
    for level in range(levels):
        level_loads[level].wait()
        if level == levels - 1:
            target = out_ref
        for box in range(boxes):
            rows = stacked(source[box], source[box ^ (1 << level)])
            target[box] = product(trans[level, box], rows)
        source, target = target, source
    level_loads[levels].wait()


def chip_kernel(own_ref, other_ref, trans_ref, *out_refs):
    own = own_place()
    for r in (1, 2, 3, 0):
        base = first_box(own ^ r)
        for q in range(4):
            for i0 in range(2):
                box = base + q * 8 + i0
                rows = stacked(own_ref[box], other_ref[box])
                out_refs[r][q, i0] = product(trans_ref[box], rows)


def quad_kernel(rank, box0, box1, box2, box3, pair_ref, keep_ref, send_ref, middle):
    boxes = (box0, box1, box2, box3)
    own, half = own_place(), own_half()
    for r in range(4):
        for q in range(4):
            for i0 in range(2):
                rows = stacked(boxes[r][q, i0], boxes[r ^ 1][q, i0])
                middle[r, q, i0] = product(pair_ref[own ^ r, q, i0, pl.ds(0, rank)], rows)
    for out_ref, bit in ((send_ref, 1 - half), (keep_ref, half)):
        for r in range(4):
            for q in range(4):
                rows = stacked(middle[r, q, bit], middle[r ^ 2, q, bit])
                out_ref[r, q] = product(pair_ref[own ^ r, q, bit, pl.ds(rank, rank)], rows)


def merge_kernel(stay_ref, late_ref, *out_refs):
    for r in range(4):
        out_refs[r][0] = stay_ref[r]
        out_refs[r][1] = late_ref[r]


def last_kernel(rank, keep_ref, recv_ref, trans0, trans1, trans2, trans3, own_ref, send_ref):
    trans = (trans0, trans1, trans2, trans3)
    core = lax.axis_index("rhs")
    for out_ref, bit in ((send_ref, 1 - core), (own_ref, core)):
        tile = []
        for side in range(2):
            for r in range(4):
                spots = trans[r][side, pl.ds(4 * rank, TILE), :]
                tile += pick(spots.astype(jnp.float32), 0, 2, 2, bit)
                for i4 in range(2):
                    q = i4 * 2 + bit
                    sides = (keep_ref[r, q], recv_ref[r, q])
                    rows = stacked(sides[side], sides[1 - side])
                    start = pl.multiple_of(q * rank, TILE)
                    index = side * 8 + r * 2 + i4
                    matrix = trans[r][side, pl.ds(start, rank), :]
                    out_ref[pl.ds(index * rank, rank), :] = product(matrix, rows)
        out_ref[pl.ds(16 * rank, TILE), :] = jnp.concatenate(tile, axis=0).astype(BF16)


def output_kernel(rank, box_ref, basis_ref, *refs):
    out_ref, result, sem = refs[-3:]
    spots = box_ref[pl.ds(16 * rank, TILE), :].astype(jnp.float32)
    copies = []
    for index in range(16):
        spot = jnp.max(spots[index : index + 1]).astype(jnp.int32)
        result[index] = lax.dot_general(
            basis_ref[spot],
            box_ref[pl.ds(index * rank, rank), :],
            (((0,), (0,)), ((), ())),
            preferred_element_type=jnp.float32,
        ).astype(BF16)
        copy = pltpu.make_async_copy(result.at[index], out_ref.at[spot], sem)
        copy.start()
        copies.append(copy)
    for copy in copies:
        copy.wait()


def call(kernel, out_shapes, in_spaces, out_spaces, scratch, flops, moved, aliases=None):
    run = pl.pallas_call(
        kernel,
        out_shape=out_shapes,
        in_specs=[pl.BlockSpec(memory_space=space) for space in in_spaces],
        out_specs=jax.tree.map(lambda space: pl.BlockSpec(memory_space=space), out_spaces),
        scratch_shapes=scratch,
        input_output_aliases=aliases or {},
        compiler_params=pltpu.CompilerParams(vmem_limit_bytes=VMEM_LIMIT),
        cost_estimate=pl.CostEstimate(flops=flops, bytes_accessed=moved, transcendentals=0),
    )

    def placed(*operands):
        return run(
            *(
                pltpu.with_memory_space_constraint(operand, space) if space == pltpu.HBM else operand
                for operand, space in zip(operands, in_spaces)
            )
        )

    return placed


def shape(*dims):
    return jax.ShapeDtypeStruct(dims, BF16)


def bind(kernel, *values):
    return lambda *refs: kernel(*values, *refs)


def move_early(right_sides, leaf_basis, translations, node_target, out_basis):
    boxes, rank, leaf_rows = leaf_basis.shape
    columns = right_sides.shape[1]
    local_levels = boxes.bit_length() - 1
    width = 2 * rank
    block = 2 * rank * columns * 2
    hbm, vmem, smem, dma = pltpu.HBM, pltpu.VMEM, pltpu.SMEM, pltpu.SemaphoreType.DMA
    quads = [[first + 2 * place for place in range(4)] for first in (0, 1, 8, 9)]

    def among_places(value):
        return lax.all_to_all(value, AXES, 0, 0, axis_index_groups=quads, tiled=True)

    def across(value, mask):
        return lax.ppermute(value, AXES, [(s, s ^ mask) for s in range(16)])

    pair, stay, late = call(
        bind(pack_kernel, rank),
        (
            shape(4, 4, 2, 2 * rank, width),
            shape(4, 4 * rank + TILE, width),
            shape(4, 4 * rank + TILE, width),
        ),
        (hbm, hbm),
        (vmem, vmem, vmem),
        [smem((boxes,), jnp.int32), dma, dma],
        0,
        3 * 2**20,
    )(node_target, translations.reshape(4, 2, 2, 2, -1, width))
    right_sides, pair, late = lax.optimization_barrier((right_sides, pair, late))
    pair = among_places(pair)
    late = across(late, 8)
    coefficients, chip_translations = call(
        bind(local_kernel, local_levels),
        (shape(boxes, rank, columns), shape(boxes, rank, width)),
        (hbm, hbm, hbm),
        (vmem, vmem),
        [
            vmem((boxes, leaf_rows, columns), BF16),
            vmem((boxes, rank, leaf_rows), BF16),
            vmem((local_levels, boxes, rank, width), BF16),
            vmem((boxes, rank, columns), BF16),
            vmem((boxes, rank, columns), BF16),
            dma((4, 2)),
            dma((local_levels + 1,)),
        ],
        boxes * rank * columns * 2 * (leaf_rows + local_levels * width),
        6 * 2**20,
    )(right_sides.reshape(boxes, leaf_rows, columns), leaf_basis, translations)
    partner = across(coefficients, 1)
    slots = call(
        chip_kernel,
        (shape(4, 2, rank, columns),) * 4,
        (vmem,) * 3,
        (vmem,) * 4,
        [],
        boxes * block * width,
        2**21,
    )(coefficients, partner, chip_translations)
    slots = [slots[0]] + [across(slots[r], 2 * r) for r in (1, 2, 3)]
    stay, late, _ = lax.optimization_barrier((stay, late, slots[1]))
    last = call(
        merge_kernel,
        (shape(2, 4 * rank + TILE, width),) * 4,
        (vmem,) * 2,
        (vmem,) * 4,
        [],
        0,
        2**20,
    )(stay, late)
    slots, last = lax.optimization_barrier((slots, last))
    keep, send = call(
        bind(quad_kernel, rank),
        (shape(4, 4, rank, columns), shape(4, 4, rank, columns)),
        (vmem,) * 5,
        (vmem,) * 2,
        [vmem((4, 4, 2, rank, columns), BF16)],
        2 * boxes * block * width,
        2**21,
    )(*slots, pair)
    received = across(send, 8)
    last = [last[0]] + [across(last[r], 2 * r) for r in (1, 2, 3)]
    own, send = call(
        bind(last_kernel, rank),
        (shape(16 * rank + TILE, columns),) * 2,
        (vmem,) * 6,
        (vmem,) * 2,
        [],
        boxes * block * width,
        2**21,
    )(keep, received, *last)
    partner = across(send, 1)
    applied = None
    for part in (own, partner):
        before = () if applied is None else (applied,)
        applied = call(
            bind(output_kernel, rank),
            shape(boxes, leaf_rows, columns),
            (vmem, vmem) + (hbm,) * len(before),
            hbm,
            [vmem((16, leaf_rows, columns), BF16), dma],
            boxes * block * width,
            2**21,
            {2: 0} if before else None,
        )(part, out_basis, *before)
    return applied.reshape(boxes * leaf_rows, columns)


def solution(mesh):
    in_specs = (
        P(("groups", "bfly", "rhs"), None),
        P(("bfly", "rhs"), None, None),
        P(("bfly", "rhs"), None, None, None),
        P(("bfly", "rhs")),
        P(("bfly", "rhs"), None, None),
    )
    out_specs = P(("groups", "bfly", "rhs"), None)

    def per_device(right_sides, leaf_basis, translations, node_target, out_basis):
        devices = lax.axis_size(AXES)
        fits = devices == 16 and leaf_basis.shape[0] == 32
        apply = move_early if fits else exchange_every_level
        return apply(right_sides, leaf_basis, translations, node_target, out_basis)

    return jax.shard_map(
        per_device, mesh=mesh, in_specs=in_specs, out_specs=out_specs, check_vma=False
    )
```

```python
import jax
import jax.numpy as jnp
from jax import lax
from jax.experimental import pallas as pl
from jax.experimental.pallas import tpu as pltpu
from jax.sharding import PartitionSpec as P

AXES = ("bfly", "rhs")
BF16 = jnp.bfloat16
TILE = 16
VMEM_LIMIT = 12 * 2**20


def from_partner(value, axis, distance):
    mask = 2**distance
    pairs = [(source, source ^ mask) for source in range(lax.axis_size(axis))]
    return lax.ppermute(value, axis, pairs)


def combine(current, partner_part, matrices):
    width = current.shape[1]
    own_term = jnp.einsum(
        "bij,bjc->bic", matrices[:, :, :width], current, preferred_element_type=jnp.float32
    )
    other_term = jnp.einsum(
        "bij,bjc->bic", matrices[:, :, width:], partner_part, preferred_element_type=jnp.float32
    )
    return (own_term + other_term).astype(BF16)


def pack_slots(flat_coefficients, slot_key, capacity, slot_total, target_spot):
    box_count = flat_coefficients.shape[0]
    box_iota = jnp.arange(box_count, dtype=jnp.int32)
    earlier = (slot_key[:, None] == slot_key[None, :]) & (box_iota[None, :] < box_iota[:, None])
    order_within = jnp.sum(earlier.astype(jnp.int32), axis=1)
    slot_of_box = slot_key * capacity + order_within
    selector = jnp.arange(slot_total, dtype=jnp.int32)[:, None] == slot_of_box[None, :]
    outgoing = jnp.dot(
        selector.astype(BF16), flat_coefficients, preferred_element_type=jnp.float32
    ).astype(BF16)
    outgoing_spot = jnp.sum(jnp.where(selector, target_spot[None, :] + 1, 0), axis=1) - 1
    return (outgoing, outgoing_spot)


def exchange_every_level(right_sides, leaf_basis, translations, node_target, out_basis):
    box_count = leaf_basis.shape[0]
    rank_width = leaf_basis.shape[1]
    leaf_rows = leaf_basis.shape[2]
    column_count = right_sides.shape[1]
    point_rows = right_sides.reshape(box_count, leaf_rows, column_count)
    coefficients = jnp.einsum(
        "brl,blc->brc", leaf_basis, point_rows, preferred_element_type=jnp.float32
    ).astype(BF16)
    local_levels = box_count.bit_length() - 1
    for level_index in range(local_levels):
        span = 2**level_index
        blocks = coefficients.reshape(box_count // (2 * span), 2, span, rank_width, column_count)
        partner_part = jnp.flip(blocks, 1).reshape(box_count, rank_width, column_count)
        coefficients = combine(coefficients, partner_part, translations[:, level_index])
    device_count = lax.axis_size(AXES)
    device_levels = device_count.bit_length() - 1
    for section_index in range(device_levels):
        partner_part = from_partner(coefficients, AXES, section_index)
        coefficients = combine(
            coefficients, partner_part, translations[:, local_levels + section_index]
        )
    target_device = node_target // box_count
    target_spot = node_target % box_count
    box_iota = jnp.arange(box_count, dtype=jnp.int32)
    flat_coefficients = coefficients.reshape(box_count, rank_width * column_count)
    capacity = max(1, box_count // device_count)
    slot_total = device_count * capacity
    outgoing, outgoing_spot = pack_slots(
        flat_coefficients, target_device, capacity, slot_total, target_spot
    )
    incoming, incoming_spot = (
        lax.all_to_all(outgoing, AXES, split_axis=0, concat_axis=0, tiled=True),
        lax.all_to_all(outgoing_spot, AXES, split_axis=0, concat_axis=0, tiled=True),
    )
    placement_table = (box_iota[:, None] == incoming_spot[None, :]).astype(BF16)
    placed = jnp.dot(placement_table, incoming, preferred_element_type=jnp.float32).astype(BF16)
    placed = placed.reshape(box_count, rank_width, column_count)
    applied = jnp.einsum("brl,brc->blc", out_basis, placed, preferred_element_type=jnp.float32)
    return applied.astype(BF16).reshape(box_count * leaf_rows, column_count)


def product(matrix, rows):
    return jnp.dot(matrix, rows, preferred_element_type=jnp.float32).astype(BF16)


def stacked(first, second):
    return jnp.concatenate([first, second], axis=0)


def own_half():
    return lax.axis_index("bfly") // 4


def own_place():
    return lax.axis_index("bfly") % 4


def first_box(place):
    return (place % 2) * 4 + (place // 2) * 2


def level_rows(trans_ref, rank, i4, place, i0, level, count):
    return trans_ref.at[i4, :, place % 2, place // 2, i0, pl.ds(level * rank, count * rank)]


def start_all(pairs, sem):
    copies = [pltpu.make_async_copy(source, target, sem) for source, target in pairs]
    for copy in copies:
        copy.start()
    return copies


BOTH = pl.ds(0, 2)


def last_level(rank, trans_ref, i4, r, side, rows_ref):
    slots = rows_ref.reshape(2, rank, trans_ref.shape[-1])
    return level_rows(trans_ref, rank, i4, own_place() ^ r, own_half() ^ side, 8, 1), slots


def spot_tile(target, i4, r, side, columns):
    first = lax.broadcasted_iota(jnp.int32, (TILE, columns), 0) == 0
    box = i4 * 16 + first_box(own_place() ^ r) + (own_half() ^ side)
    return jnp.where(first, target[box] % 32, target[box + 8] % 32).astype(jnp.float32).astype(BF16)


def pack_kernel(rank, target_ref, trans_ref, *refs):
    out_refs, (target, sem, target_sem) = refs[:3], refs[3:]
    group, columns = lax.axis_index("groups"), trans_ref.shape[-1]
    target_copy = pltpu.make_async_copy(target_ref, target, target_sem)
    target_copy.start()
    pairs = []
    for r in (3, 2, 1):
        ref = out_refs[r - 1]
        slots = ref.at[pl.ds(0, 8 * rank)].reshape(2, 2, 2 * rank, columns)
        pairs.append((level_rows(trans_ref, rank, group, own_place() ^ r, BOTH, 6, 2), slots))
        pairs.append(last_level(rank, trans_ref, group, r, 0, ref.at[pl.ds(8 * rank, 2 * rank)]))
    copies = start_all(pairs, sem)
    target_copy.wait()
    for r in (3, 2, 1):
        out_refs[r - 1][pl.ds(10 * rank, TILE), :] = spot_tile(target, group, r, 0, columns)
    for copy in copies:
        copy.wait()


def gather_kernel(near1, near2, near3, out_ref):
    for index, ref in enumerate((near1, near2, near3)):
        out_ref[index] = ref[...]


def local_kernel(
    levels, rs_ref, leaf_ref, trans_ref, grid_ref, target_ref, out_ref, next_ref, pair_ref, stay_ref, late_ref,
    rs, leaf, trans, ping, pong, target_smem, sem, trans_sem, rest_sem, target_sem
):
    rank = leaf_ref.shape[1]
    target_copy = pltpu.make_async_copy(target_ref, target_smem, target_sem)
    target_copy.start()
    boxes = leaf_ref.shape[0]
    step = boxes // 4
    loads = []
    for part in range(4):
        rows = pl.ds(part * step, step)
        loads.append(
            (
                pltpu.make_async_copy(rs_ref.at[rows], rs.at[rows], sem.at[part, 0]),
                pltpu.make_async_copy(leaf_ref.at[rows], leaf.at[rows], sem.at[part, 1]),
            )
        )
    level_loads = [
        pltpu.make_async_copy(trans_ref.at[:, level], trans.at[level], trans_sem.at[level])
        for level in range(levels)
    ]
    level_loads.append(
        pltpu.make_async_copy(trans_ref.at[:, levels], next_ref, trans_sem.at[levels])
    )
    for pair in loads:
        for copy in pair:
            copy.start()
    for copy in level_loads:
        copy.start()
    group, columns = lax.axis_index("groups"), grid_ref.shape[-1]
    rest = [(level_rows(grid_ref, rank, BOTH, own_place(), BOTH, 6, 2), pair_ref)]
    two = pl.ds(0, 2 * rank)
    rest += [last_level(rank, grid_ref, i4, 0, 0, stay_ref.at[i4, two]) for i4 in range(2)]
    rest += [last_level(rank, grid_ref, group, r, 1, late_ref.at[r, two]) for r in range(4)]
    rest = start_all(rest, rest_sem)
    target_copy.wait()
    tile = pl.ds(2 * rank, TILE)
    for i4 in range(2):
        stay_ref[i4, tile, :] = spot_tile(target_smem, i4, 0, 0, columns)
    for r in range(4):
        late_ref[r, tile, :] = spot_tile(target_smem, group, r, 1, columns)
    for part in range(4):
        for copy in loads[part]:
            copy.wait()
        for box in range(part * step, (part + 1) * step):
            ping[box] = product(leaf[box], rs[box])
    source, target = ping, pong
    for level in range(levels):
        level_loads[level].wait()
        if level == levels - 1:
            target = out_ref
        for box in range(boxes):
            rows = stacked(source[box], source[box ^ (1 << level)])
            target[box] = product(trans[level, box], rows)
        source, target = target, source
    level_loads[levels].wait()
    for copy in rest:
        copy.wait()


def chip_kernel(own_ref, other_ref, trans_ref, *out_refs):
    own = own_place()
    for r in (1, 2, 3, 0):
        base = first_box(own ^ r)
        for q in range(4):
            for i0 in range(2):
                box = base + q * 8 + i0
                rows = stacked(own_ref[box], other_ref[box])
                out_refs[r][q, i0] = product(trans_ref[box], rows)


def quad_kernel(
    rank, box0, box1, box2, box3, pair_ref, near1, near2, near3, far_ref, keep_ref, send_ref, middle
):
    boxes = (box0, box1, box2, box3)
    half, group = own_half(), lax.axis_index("groups")

    def matrix(r, h, i3, i0, level):
        if r == 0:
            return pair_ref[group ^ h, i3, i0, pl.ds(level * rank, rank)]
        ref = far_ref.at[r - 1] if h else (near1, near2, near3)[r - 1]
        start = pl.multiple_of(((i3 * 2 + i0) * 2 + level) * rank, TILE)
        return ref[pl.ds(start, rank), :]

    order = [(r, h, i3) for r in range(4) for h in range(2) for i3 in range(2)]
    for r, h, i3 in order:
        q = (group ^ h) * 2 + i3
        for i0 in range(2):
            rows = stacked(boxes[r][q, i0], boxes[r ^ 1][q, i0])
            middle[r, q, i0] = product(matrix(r, h, i3, i0, 0), rows)
    for out_ref, bit in ((send_ref, 1 - half), (keep_ref, half)):
        for r, h, i3 in order:
            q = (group ^ h) * 2 + i3
            rows = stacked(middle[r, q, bit], middle[r ^ 2, q, bit])
            out_ref[r, q] = product(matrix(r, h, i3, bit, 1), rows)


def split_kernel(late_ref, *out_refs):
    for r in range(4):
        out_refs[r][...] = late_ref[r]


def collect_kernel(late0, late1, late2, late3, out_ref):
    for r, ref in enumerate((late0, late1, late2, late3)):
        out_ref[r] = ref[...]


def last_kernel(
    rank, keep_ref, recv_ref, stay_ref, near1, near2, near3, far_ref, here_ref, cross_ref, own_ref, send_ref
):
    group, core = lax.axis_index("groups"), lax.axis_index("rhs")

    def source(side, r, h):
        if side:
            return (here_ref, cross_ref)[h].at[r], 0
        if r == 0:
            return stay_ref.at[group ^ h], 0
        return (far_ref.at[r - 1] if h else (near1, near2, near3)[r - 1]), 8 * rank

    for out_ref, bit in ((send_ref, 1 - core), (own_ref, core)):
        tile = []
        for side in range(2):
            for r in range(4):
                for h in range(2):
                    ref, base = source(side, r, h)
                    spots = ref[pl.ds(base + 2 * rank, TILE), :].astype(jnp.float32)
                    tile.append(jnp.where(bit == 0, spots[0:1], spots[1:2]))
                    q = (group ^ h) * 2 + bit
                    sides = (keep_ref[r, q], recv_ref[r, q])
                    rows = stacked(sides[side], sides[1 - side])
                    start = pl.multiple_of(base + bit * rank, TILE)
                    index = side * 8 + r * 2 + h
                    out_ref[pl.ds(index * rank, rank), :] = product(ref[pl.ds(start, rank), :], rows)
        out_ref[pl.ds(16 * rank, TILE), :] = jnp.concatenate(tile, axis=0).astype(BF16)


def output_kernel(rank, box_ref, basis_ref, *refs):
    out_ref, result, sem = refs[-3:]
    spots = box_ref[pl.ds(16 * rank, TILE), :].astype(jnp.float32)
    copies = []
    for index in range(16):
        spot = jnp.max(spots[index : index + 1]).astype(jnp.int32)
        result[index] = lax.dot_general(
            basis_ref[spot],
            box_ref[pl.ds(index * rank, rank), :],
            (((0,), (0,)), ((), ())),
            preferred_element_type=jnp.float32,
        ).astype(BF16)
        copy = pltpu.make_async_copy(result.at[index], out_ref.at[spot], sem)
        copy.start()
        copies.append(copy)
    for copy in copies:
        copy.wait()


def call(kernel, out_shapes, in_spaces, out_spaces, scratch, flops, moved, aliases=None):
    run = pl.pallas_call(
        kernel,
        out_shape=out_shapes,
        in_specs=[pl.BlockSpec(memory_space=space) for space in in_spaces],
        out_specs=jax.tree.map(lambda space: pl.BlockSpec(memory_space=space), out_spaces),
        scratch_shapes=scratch,
        input_output_aliases=aliases or {},
        compiler_params=pltpu.CompilerParams(vmem_limit_bytes=VMEM_LIMIT),
        cost_estimate=pl.CostEstimate(flops=flops, bytes_accessed=moved, transcendentals=0),
    )

    def placed(*operands):
        return run(
            *(
                pltpu.with_memory_space_constraint(operand, space) if space == pltpu.HBM else operand
                for operand, space in zip(operands, in_spaces)
            )
        )

    return placed


def shape(*dims):
    return jax.ShapeDtypeStruct(dims, BF16)


def bind(kernel, *values):
    return lambda *refs: kernel(*values, *refs)


def move_early(right_sides, leaf_basis, translations, node_target, out_basis):
    boxes, rank, leaf_rows = leaf_basis.shape
    columns = right_sides.shape[1]
    local_levels = boxes.bit_length() - 1
    width = 2 * rank
    block = 2 * rank * columns * 2
    hbm, vmem, smem, dma = pltpu.HBM, pltpu.VMEM, pltpu.SMEM, pltpu.SemaphoreType.DMA
    def across(value, mask):
        return lax.ppermute(value, AXES, [(s, s ^ mask) for s in range(16)])

    def swapped(value):
        return lax.ppermute(value, "groups", [(0, 1), (1, 0)])

    grid = translations.reshape(2, 2, 2, 2, 2, -1, width)
    part = shape(2 * rank + TILE, width)
    near_part = shape(10 * rank + TILE, width)
    near = call(
        bind(pack_kernel, rank),
        (near_part,) * 3,
        (hbm, hbm),
        (vmem,) * 3,
        [smem((boxes,), jnp.int32), dma, dma],
        0,
        2**20,
    )(node_target, grid)
    right_sides, near = lax.optimization_barrier((right_sides, near))
    near = [across(near[r - 1], 2 * r) for r in (1, 2, 3)]
    coefficients, chip_translations, own_pair, stay, late = call(
        bind(local_kernel, local_levels),
        (
            shape(boxes, rank, columns),
            shape(boxes, rank, width),
            shape(2, 2, 2, 2 * rank, width),
            shape(2, *part.shape),
            shape(4, *part.shape),
        ),
        (hbm,) * 5,
        (vmem,) * 5,
        [
            vmem((boxes, leaf_rows, columns), BF16),
            vmem((boxes, rank, leaf_rows), BF16),
            vmem((local_levels, boxes, rank, width), BF16),
            vmem((boxes, rank, columns), BF16),
            vmem((boxes, rank, columns), BF16),
            smem((boxes,), jnp.int32),
            dma((4, 2)),
            dma((local_levels + 1,)),
            dma,
            dma,
        ],
        boxes * rank * columns * 2 * (leaf_rows + local_levels * width),
        6 * 2**20,
    )(
        right_sides.reshape(boxes, leaf_rows, columns), leaf_basis, translations, grid, node_target
    )
    late = across(late, 8)
    coefficients, near = lax.optimization_barrier((coefficients, near))
    partner = across(coefficients, 1)
    far = call(gather_kernel, shape(3, *near_part.shape), (vmem,) * 3, vmem, [], 0, 2**20)(*near)
    partner, _ = lax.optimization_barrier((partner, far))
    far = swapped(far)
    slots = call(
        chip_kernel,
        (shape(4, 2, rank, columns),) * 4,
        (vmem,) * 3,
        (vmem,) * 4,
        [],
        boxes * block * width,
        2**21,
    )(coefficients, partner, chip_translations)
    slots = [slots[0]] + [across(slots[r], 2 * r) for r in (1, 2, 3)]
    late, *_ = lax.optimization_barrier((late, slots[1]))
    late = call(split_kernel, (part,) * 4, (vmem,), (vmem,) * 4, [], 0, 2**20)(late)
    late = [late[0]] + [across(late[r], 2 * r) for r in (1, 2, 3)]
    here = call(collect_kernel, shape(4, *part.shape), (vmem,) * 4, vmem, [], 0, 2**20)(*late)
    keep, send = call(
        bind(quad_kernel, rank),
        (shape(4, 4, rank, columns), shape(4, 4, rank, columns)),
        (vmem,) * 9,
        (vmem,) * 2,
        [vmem((4, 4, 2, rank, columns), BF16)],
        2 * boxes * block * width,
        2**21,
    )(*slots, own_pair, *near, far)
    received = across(send, 8)
    here, _ = lax.optimization_barrier((here, send))
    cross = swapped(here)
    own, send = call(
        bind(last_kernel, rank),
        (shape(16 * rank + TILE, columns),) * 2,
        (vmem,) * 9,
        (vmem,) * 2,
        [],
        boxes * block * width,
        2**21,
    )(keep, received, stay, *near, far, here, cross)
    partner = across(send, 1)
    applied = None
    for part in (own, partner):
        before = () if applied is None else (applied,)
        applied = call(
            bind(output_kernel, rank),
            shape(boxes, leaf_rows, columns),
            (vmem, vmem) + (hbm,) * len(before),
            hbm,
            [vmem((16, leaf_rows, columns), BF16), dma],
            boxes * block * width,
            2**21,
            {2: 0} if before else None,
        )(part, out_basis, *before)
    return applied.reshape(boxes * leaf_rows, columns)


def solution(mesh):
    in_specs = (
        P(("groups", "bfly", "rhs"), None),
        P(("bfly", "rhs"), None, None),
        P(("bfly", "rhs"), None, None, None),
        P(("bfly", "rhs")),
        P(("bfly", "rhs"), None, None),
    )
    out_specs = P(("groups", "bfly", "rhs"), None)

    def per_device(right_sides, leaf_basis, translations, node_target, out_basis):
        devices = lax.axis_size(AXES)
        fits = devices == 16 and lax.axis_size("groups") == 2 and leaf_basis.shape[0] == 32
        apply = move_early if fits else exchange_every_level
        return apply(right_sides, leaf_basis, translations, node_target, out_basis)

    return jax.shard_map(
        per_device, mesh=mesh, in_specs=in_specs, out_specs=out_specs, check_vma=False
    )
```

```python
import jax
import jax.numpy as jnp
from jax import lax
from jax.experimental import pallas as pl
from jax.experimental.pallas import tpu as pltpu
from jax.sharding import PartitionSpec as P

AXES = ("bfly", "rhs")
BF16 = jnp.bfloat16
TILE = 16
VMEM_LIMIT = 12 * 2**20


def from_partner(value, axis, distance):
    mask = 2**distance
    pairs = [(source, source ^ mask) for source in range(lax.axis_size(axis))]
    return lax.ppermute(value, axis, pairs)


def combine(current, partner_part, matrices):
    width = current.shape[1]
    own_term = jnp.einsum(
        "bij,bjc->bic", matrices[:, :, :width], current, preferred_element_type=jnp.float32
    )
    other_term = jnp.einsum(
        "bij,bjc->bic", matrices[:, :, width:], partner_part, preferred_element_type=jnp.float32
    )
    return (own_term + other_term).astype(BF16)


def pack_slots(flat_coefficients, slot_key, capacity, slot_total, target_spot):
    box_count = flat_coefficients.shape[0]
    box_iota = jnp.arange(box_count, dtype=jnp.int32)
    earlier = (slot_key[:, None] == slot_key[None, :]) & (box_iota[None, :] < box_iota[:, None])
    order_within = jnp.sum(earlier.astype(jnp.int32), axis=1)
    slot_of_box = slot_key * capacity + order_within
    selector = jnp.arange(slot_total, dtype=jnp.int32)[:, None] == slot_of_box[None, :]
    outgoing = jnp.dot(
        selector.astype(BF16), flat_coefficients, preferred_element_type=jnp.float32
    ).astype(BF16)
    outgoing_spot = jnp.sum(jnp.where(selector, target_spot[None, :] + 1, 0), axis=1) - 1
    return (outgoing, outgoing_spot)


def exchange_every_level(right_sides, leaf_basis, translations, node_target, out_basis):
    box_count = leaf_basis.shape[0]
    rank_width = leaf_basis.shape[1]
    leaf_rows = leaf_basis.shape[2]
    column_count = right_sides.shape[1]
    point_rows = right_sides.reshape(box_count, leaf_rows, column_count)
    coefficients = jnp.einsum(
        "brl,blc->brc", leaf_basis, point_rows, preferred_element_type=jnp.float32
    ).astype(BF16)
    local_levels = box_count.bit_length() - 1
    for level_index in range(local_levels):
        span = 2**level_index
        blocks = coefficients.reshape(box_count // (2 * span), 2, span, rank_width, column_count)
        partner_part = jnp.flip(blocks, 1).reshape(box_count, rank_width, column_count)
        coefficients = combine(coefficients, partner_part, translations[:, level_index])
    device_count = lax.axis_size(AXES)
    device_levels = device_count.bit_length() - 1
    for section_index in range(device_levels):
        partner_part = from_partner(coefficients, AXES, section_index)
        coefficients = combine(
            coefficients, partner_part, translations[:, local_levels + section_index]
        )
    target_device = node_target // box_count
    target_spot = node_target % box_count
    box_iota = jnp.arange(box_count, dtype=jnp.int32)
    flat_coefficients = coefficients.reshape(box_count, rank_width * column_count)
    capacity = max(1, box_count // device_count)
    slot_total = device_count * capacity
    outgoing, outgoing_spot = pack_slots(
        flat_coefficients, target_device, capacity, slot_total, target_spot
    )
    incoming, incoming_spot = (
        lax.all_to_all(outgoing, AXES, split_axis=0, concat_axis=0, tiled=True),
        lax.all_to_all(outgoing_spot, AXES, split_axis=0, concat_axis=0, tiled=True),
    )
    placement_table = (box_iota[:, None] == incoming_spot[None, :]).astype(BF16)
    placed = jnp.dot(placement_table, incoming, preferred_element_type=jnp.float32).astype(BF16)
    placed = placed.reshape(box_count, rank_width, column_count)
    applied = jnp.einsum("brl,brc->blc", out_basis, placed, preferred_element_type=jnp.float32)
    return applied.astype(BF16).reshape(box_count * leaf_rows, column_count)


def product(matrix, rows):
    return jnp.dot(matrix, rows, preferred_element_type=jnp.float32).astype(BF16)


def stacked(first, second):
    return jnp.concatenate([first, second], axis=0)


def own_half():
    return lax.axis_index("bfly") // 4


def own_place():
    return lax.axis_index("bfly") % 4


def first_box(place):
    return (place % 2) * 4 + (place // 2) * 2


def level_rows(trans_ref, rank, i4, place, i0, level, count):
    return trans_ref.at[i4, :, place % 2, place // 2, i0, pl.ds(level * rank, count * rank)]


def start_all(pairs, sem):
    copies = [pltpu.make_async_copy(source, target, sem) for source, target in pairs]
    for copy in copies:
        copy.start()
    return copies


BOTH = pl.ds(0, 2)


def last_level(rank, trans_ref, i4, r, side, rows_ref):
    slots = rows_ref.reshape(2, rank, trans_ref.shape[-1])
    return level_rows(trans_ref, rank, i4, own_place() ^ r, own_half() ^ side, 8, 1), slots


def spot_tile(target, i4, r, columns):
    row = lax.broadcasted_iota(jnp.int32, (TILE, columns), 0)
    base = i4 * 16 + first_box(own_place() ^ r)
    half = own_half()
    spots = [target[base + (half ^ side) + i3 * 8] % 32 for side in range(2) for i3 in range(2)]
    upper = jnp.where(row == 2, spots[2], spots[3])
    tile = jnp.where(row < 2, jnp.where(row == 0, spots[0], spots[1]), upper)
    return tile.astype(jnp.float32).astype(BF16)


def pack_kernel(rank, target_ref, trans_ref, *refs):
    out_refs, (target, sem, target_sem) = refs[:3], refs[3:]
    group, columns = lax.axis_index("groups"), trans_ref.shape[-1]
    target_copy = pltpu.make_async_copy(target_ref, target, target_sem)
    target_copy.start()
    pairs = []
    for r in (3, 2, 1):
        ref = out_refs[r - 1]
        slots = ref.at[pl.ds(0, 8 * rank)].reshape(2, 2, 2 * rank, columns)
        pairs.append((level_rows(trans_ref, rank, group, own_place() ^ r, BOTH, 6, 2), slots))
        for side in range(2):
            rows = ref.at[pl.ds((8 + 2 * side) * rank, 2 * rank)]
            pairs.append(last_level(rank, trans_ref, group, r, side, rows))
    copies = start_all(pairs, sem)
    target_copy.wait()
    for r in (3, 2, 1):
        out_refs[r - 1][pl.ds(12 * rank, TILE), :] = spot_tile(target, group, r, columns)
    for copy in copies:
        copy.wait()


def gather_kernel(rank, near1, near2, near3, out_ref):
    for index, ref in enumerate((near1, near2, near3)):
        out_ref[index, pl.ds(0, 10 * rank), :] = ref[pl.ds(0, 10 * rank), :]
        out_ref[index, pl.ds(10 * rank, TILE), :] = ref[pl.ds(12 * rank, TILE), :]


def late_kernel(rank, late_ref, near1, near2, near3, out_ref):
    out_ref[0] = late_ref[...]
    for index, ref in enumerate((near1, near2, near3)):
        out_ref[index + 1] = ref[pl.ds(10 * rank, 2 * rank + TILE), :]


def local_kernel(
    levels, rs_ref, leaf_ref, trans_ref, grid_ref, target_ref, out_ref, next_ref, pair_ref, stay_ref, late_ref,
    rs, leaf, trans, ping, pong, target_smem, sem, trans_sem, rest_sem, target_sem
):
    rank = leaf_ref.shape[1]
    target_copy = pltpu.make_async_copy(target_ref, target_smem, target_sem)
    target_copy.start()
    boxes = leaf_ref.shape[0]
    step = boxes // 4
    loads = []
    for part in range(4):
        rows = pl.ds(part * step, step)
        loads.append(
            (
                pltpu.make_async_copy(rs_ref.at[rows], rs.at[rows], sem.at[part, 0]),
                pltpu.make_async_copy(leaf_ref.at[rows], leaf.at[rows], sem.at[part, 1]),
            )
        )
    level_loads = [
        pltpu.make_async_copy(trans_ref.at[:, level], trans.at[level], trans_sem.at[level])
        for level in range(levels)
    ]
    level_loads.append(
        pltpu.make_async_copy(trans_ref.at[:, levels], next_ref, trans_sem.at[levels])
    )
    for pair in loads:
        for copy in pair:
            copy.start()
    for copy in level_loads:
        copy.start()
    group, columns = lax.axis_index("groups"), grid_ref.shape[-1]
    rest = [(level_rows(grid_ref, rank, BOTH, own_place(), BOTH, 6, 2), pair_ref)]
    two = pl.ds(0, 2 * rank)
    rest += [last_level(rank, grid_ref, i4, 0, 0, stay_ref.at[i4, two]) for i4 in range(2)]
    rest.append(last_level(rank, grid_ref, group, 0, 1, late_ref.at[two]))
    rest = start_all(rest, rest_sem)
    target_copy.wait()
    tile = pl.ds(2 * rank, TILE)
    for i4 in range(2):
        stay_ref[i4, tile, :] = spot_tile(target_smem, i4, 0, columns)
    late_ref[tile, :] = spot_tile(target_smem, group, 0, columns)
    for part in range(4):
        for copy in loads[part]:
            copy.wait()
        for box in range(part * step, (part + 1) * step):
            ping[box] = product(leaf[box], rs[box])
    source, target = ping, pong
    for level in range(levels):
        level_loads[level].wait()
        if level == levels - 1:
            target = out_ref
        for box in range(boxes):
            rows = stacked(source[box], source[box ^ (1 << level)])
            target[box] = product(trans[level, box], rows)
        source, target = target, source
    level_loads[levels].wait()
    for copy in rest:
        copy.wait()


def chip_kernel(own_ref, other_ref, trans_ref, *out_refs):
    own = own_place()
    for r in (1, 2, 3, 0):
        base = first_box(own ^ r)
        for q in range(4):
            for i0 in range(2):
                box = base + q * 8 + i0
                rows = stacked(own_ref[box], other_ref[box])
                out_refs[r][q, i0] = product(trans_ref[box], rows)


def quad_kernel(
    rank, box0, box1, box2, box3, pair_ref, near1, near2, near3, far_ref, keep_ref, send_ref, middle
):
    boxes = (box0, box1, box2, box3)
    half, group = own_half(), lax.axis_index("groups")

    def matrix(r, h, i3, i0, level):
        if r == 0:
            return pair_ref[group ^ h, i3, i0, pl.ds(level * rank, rank)]
        ref = far_ref.at[r - 1] if h else (near1, near2, near3)[r - 1]
        start = pl.multiple_of(((i3 * 2 + i0) * 2 + level) * rank, TILE)
        return ref[pl.ds(start, rank), :]

    order = [(r, h, i3) for r in range(4) for h in range(2) for i3 in range(2)]
    for r, h, i3 in order:
        q = (group ^ h) * 2 + i3
        for i0 in range(2):
            rows = stacked(boxes[r][q, i0], boxes[r ^ 1][q, i0])
            middle[r, q, i0] = product(matrix(r, h, i3, i0, 0), rows)
    for out_ref, bit in ((send_ref, 1 - half), (keep_ref, half)):
        for r, h, i3 in order:
            q = (group ^ h) * 2 + i3
            rows = stacked(middle[r, q, bit], middle[r ^ 2, q, bit])
            out_ref[r, q] = product(matrix(r, h, i3, bit, 1), rows)


def last_kernel(
    rank, keep_ref, recv_ref, stay_ref, near1, near2, near3, far_ref, here_ref, cross_ref, own_ref, send_ref
):
    group, core = lax.axis_index("groups"), lax.axis_index("rhs")

    def source(side, r, h):
        if side:
            return (here_ref, cross_ref)[h].at[r], 0, 2 * rank
        if r == 0:
            return stay_ref.at[group ^ h], 0, 2 * rank
        if h:
            return far_ref.at[r - 1], 8 * rank, 10 * rank
        return (near1, near2, near3)[r - 1], 8 * rank, 12 * rank

    for out_ref, bit in ((send_ref, 1 - core), (own_ref, core)):
        tile = []
        for side in range(2):
            for r in range(4):
                for h in range(2):
                    ref, base, at = source(side, r, h)
                    spots = ref[pl.ds(at, TILE), :].astype(jnp.float32)[2 * side : 2 * side + 2]
                    tile.append(jnp.where(bit == 0, spots[0:1], spots[1:2]))
                    q = (group ^ h) * 2 + bit
                    sides = (keep_ref[r, q], recv_ref[r, q])
                    rows = stacked(sides[side], sides[1 - side])
                    start = pl.multiple_of(base + bit * rank, TILE)
                    index = side * 8 + r * 2 + h
                    out_ref[pl.ds(index * rank, rank), :] = product(ref[pl.ds(start, rank), :], rows)
        out_ref[pl.ds(16 * rank, TILE), :] = jnp.concatenate(tile, axis=0).astype(BF16)


def output_kernel(rank, box_ref, basis_ref, *refs):
    out_ref, result, sem = refs[-3:]
    spots = box_ref[pl.ds(16 * rank, TILE), :].astype(jnp.float32)
    copies = []
    for index in range(16):
        spot = jnp.max(spots[index : index + 1]).astype(jnp.int32)
        result[index] = lax.dot_general(
            basis_ref[spot],
            box_ref[pl.ds(index * rank, rank), :],
            (((0,), (0,)), ((), ())),
            preferred_element_type=jnp.float32,
        ).astype(BF16)
        copy = pltpu.make_async_copy(result.at[index], out_ref.at[spot], sem)
        copy.start()
        copies.append(copy)
    for copy in copies:
        copy.wait()


def call(kernel, out_shapes, in_spaces, out_spaces, scratch, flops, moved, aliases=None):
    run = pl.pallas_call(
        kernel,
        out_shape=out_shapes,
        in_specs=[pl.BlockSpec(memory_space=space) for space in in_spaces],
        out_specs=jax.tree.map(lambda space: pl.BlockSpec(memory_space=space), out_spaces),
        scratch_shapes=scratch,
        input_output_aliases=aliases or {},
        compiler_params=pltpu.CompilerParams(vmem_limit_bytes=VMEM_LIMIT),
        cost_estimate=pl.CostEstimate(flops=flops, bytes_accessed=moved, transcendentals=0),
    )

    def placed(*operands):
        return run(
            *(
                pltpu.with_memory_space_constraint(operand, space) if space == pltpu.HBM else operand
                for operand, space in zip(operands, in_spaces)
            )
        )

    return placed


def shape(*dims):
    return jax.ShapeDtypeStruct(dims, BF16)


def bind(kernel, *values):
    return lambda *refs: kernel(*values, *refs)


def move_early(right_sides, leaf_basis, translations, node_target, out_basis):
    boxes, rank, leaf_rows = leaf_basis.shape
    columns = right_sides.shape[1]
    local_levels = boxes.bit_length() - 1
    width = 2 * rank
    block = 2 * rank * columns * 2
    hbm, vmem, smem, dma = pltpu.HBM, pltpu.VMEM, pltpu.SMEM, pltpu.SemaphoreType.DMA
    def across(value, mask):
        return lax.ppermute(value, AXES, [(s, s ^ mask) for s in range(16)])

    def swapped(value):
        return lax.ppermute(value, "groups", [(0, 1), (1, 0)])

    grid = translations.reshape(2, 2, 2, 2, 2, -1, width)
    part = shape(2 * rank + TILE, width)
    near_part = shape(12 * rank + TILE, width)
    near = call(
        bind(pack_kernel, rank),
        (near_part,) * 3,
        (hbm, hbm),
        (vmem,) * 3,
        [smem((boxes,), jnp.int32), dma, dma],
        0,
        2**20,
    )(node_target, grid)
    right_sides, near = lax.optimization_barrier((right_sides, near))
    near = [across(near[r - 1], 2 * r) for r in (1, 2, 3)]
    coefficients, chip_translations, own_pair, stay, late = call(
        bind(local_kernel, local_levels),
        (
            shape(boxes, rank, columns),
            shape(boxes, rank, width),
            shape(2, 2, 2, 2 * rank, width),
            shape(2, *part.shape),
            part,
        ),
        (hbm,) * 5,
        (vmem,) * 5,
        [
            vmem((boxes, leaf_rows, columns), BF16),
            vmem((boxes, rank, leaf_rows), BF16),
            vmem((local_levels, boxes, rank, width), BF16),
            vmem((boxes, rank, columns), BF16),
            vmem((boxes, rank, columns), BF16),
            smem((boxes,), jnp.int32),
            dma((4, 2)),
            dma((local_levels + 1,)),
            dma,
            dma,
        ],
        boxes * rank * columns * 2 * (leaf_rows + local_levels * width),
        6 * 2**20,
    )(
        right_sides.reshape(boxes, leaf_rows, columns), leaf_basis, translations, grid, node_target
    )
    coefficients, near = lax.optimization_barrier((coefficients, near))
    partner = across(coefficients, 1)
    far = call(bind(gather_kernel, rank), shape(3, 10 * rank + TILE, width), (vmem,) * 3, vmem, [], 0, 2**20)(*near)
    partner, _ = lax.optimization_barrier((partner, far))
    far = swapped(far)
    slots = call(
        chip_kernel,
        (shape(4, 2, rank, columns),) * 4,
        (vmem,) * 3,
        (vmem,) * 4,
        [],
        boxes * block * width,
        2**21,
    )(coefficients, partner, chip_translations)
    slots = [slots[0]] + [across(slots[r], 2 * r) for r in (1, 2, 3)]
    _, late = lax.optimization_barrier((slots[1], late))
    here = call(
        bind(late_kernel, rank), shape(4, *part.shape), (vmem,) * 4, vmem, [], 0, 2**20
    )(late, *near)
    here = across(here, 8)
    keep, send = call(
        bind(quad_kernel, rank),
        (shape(4, 4, rank, columns), shape(4, 4, rank, columns)),
        (vmem,) * 9,
        (vmem,) * 2,
        [vmem((4, 4, 2, rank, columns), BF16)],
        2 * boxes * block * width,
        2**21,
    )(*slots, own_pair, *near, far)
    received = across(send, 8)
    here, _ = lax.optimization_barrier((here, send))
    cross = swapped(here)
    own, send = call(
        bind(last_kernel, rank),
        (shape(16 * rank + TILE, columns),) * 2,
        (vmem,) * 9,
        (vmem,) * 2,
        [],
        boxes * block * width,
        2**21,
    )(keep, received, stay, *near, far, here, cross)
    partner = across(send, 1)
    applied = None
    for part in (own, partner):
        before = () if applied is None else (applied,)
        applied = call(
            bind(output_kernel, rank),
            shape(boxes, leaf_rows, columns),
            (vmem, vmem) + (hbm,) * len(before),
            hbm,
            [vmem((16, leaf_rows, columns), BF16), dma],
            boxes * block * width,
            2**21,
            {2: 0} if before else None,
        )(part, out_basis, *before)
    return applied.reshape(boxes * leaf_rows, columns)


def solution(mesh):
    in_specs = (
        P(("groups", "bfly", "rhs"), None),
        P(("bfly", "rhs"), None, None),
        P(("bfly", "rhs"), None, None, None),
        P(("bfly", "rhs")),
        P(("bfly", "rhs"), None, None),
    )
    out_specs = P(("groups", "bfly", "rhs"), None)

    def per_device(right_sides, leaf_basis, translations, node_target, out_basis):
        devices = lax.axis_size(AXES)
        fits = devices == 16 and lax.axis_size("groups") == 2 and leaf_basis.shape[0] == 32
        apply = move_early if fits else exchange_every_level
        return apply(right_sides, leaf_basis, translations, node_target, out_basis)

    return jax.shard_map(
        per_device, mesh=mesh, in_specs=in_specs, out_specs=out_specs, check_vma=False
    )
```

```python
import jax
import jax.numpy as jnp
from jax import lax
from jax.experimental import pallas as pl
from jax.experimental.pallas import tpu as pltpu
from jax.sharding import PartitionSpec as P

AXES = ("bfly", "rhs")
BF16 = jnp.bfloat16
TILE = 16
VMEM_LIMIT = 12 * 2**20


def from_partner(value, axis, distance):
    mask = 2**distance
    pairs = [(source, source ^ mask) for source in range(lax.axis_size(axis))]
    return lax.ppermute(value, axis, pairs)


def combine(current, partner_part, matrices):
    width = current.shape[1]
    own_term = jnp.einsum(
        "bij,bjc->bic", matrices[:, :, :width], current, preferred_element_type=jnp.float32
    )
    other_term = jnp.einsum(
        "bij,bjc->bic", matrices[:, :, width:], partner_part, preferred_element_type=jnp.float32
    )
    return (own_term + other_term).astype(BF16)


def pack_slots(flat_coefficients, slot_key, capacity, slot_total, target_spot):
    box_count = flat_coefficients.shape[0]
    box_iota = jnp.arange(box_count, dtype=jnp.int32)
    earlier = (slot_key[:, None] == slot_key[None, :]) & (box_iota[None, :] < box_iota[:, None])
    order_within = jnp.sum(earlier.astype(jnp.int32), axis=1)
    slot_of_box = slot_key * capacity + order_within
    selector = jnp.arange(slot_total, dtype=jnp.int32)[:, None] == slot_of_box[None, :]
    outgoing = jnp.dot(
        selector.astype(BF16), flat_coefficients, preferred_element_type=jnp.float32
    ).astype(BF16)
    outgoing_spot = jnp.sum(jnp.where(selector, target_spot[None, :] + 1, 0), axis=1) - 1
    return (outgoing, outgoing_spot)


def exchange_every_level(right_sides, leaf_basis, translations, node_target, out_basis):
    box_count = leaf_basis.shape[0]
    rank_width = leaf_basis.shape[1]
    leaf_rows = leaf_basis.shape[2]
    column_count = right_sides.shape[1]
    point_rows = right_sides.reshape(box_count, leaf_rows, column_count)
    coefficients = jnp.einsum(
        "brl,blc->brc", leaf_basis, point_rows, preferred_element_type=jnp.float32
    ).astype(BF16)
    local_levels = box_count.bit_length() - 1
    for level_index in range(local_levels):
        span = 2**level_index
        blocks = coefficients.reshape(box_count // (2 * span), 2, span, rank_width, column_count)
        partner_part = jnp.flip(blocks, 1).reshape(box_count, rank_width, column_count)
        coefficients = combine(coefficients, partner_part, translations[:, level_index])
    device_count = lax.axis_size(AXES)
    device_levels = device_count.bit_length() - 1
    for section_index in range(device_levels):
        partner_part = from_partner(coefficients, AXES, section_index)
        coefficients = combine(
            coefficients, partner_part, translations[:, local_levels + section_index]
        )
    target_device = node_target // box_count
    target_spot = node_target % box_count
    box_iota = jnp.arange(box_count, dtype=jnp.int32)
    flat_coefficients = coefficients.reshape(box_count, rank_width * column_count)
    capacity = max(1, box_count // device_count)
    slot_total = device_count * capacity
    outgoing, outgoing_spot = pack_slots(
        flat_coefficients, target_device, capacity, slot_total, target_spot
    )
    incoming, incoming_spot = (
        lax.all_to_all(outgoing, AXES, split_axis=0, concat_axis=0, tiled=True),
        lax.all_to_all(outgoing_spot, AXES, split_axis=0, concat_axis=0, tiled=True),
    )
    placement_table = (box_iota[:, None] == incoming_spot[None, :]).astype(BF16)
    placed = jnp.dot(placement_table, incoming, preferred_element_type=jnp.float32).astype(BF16)
    placed = placed.reshape(box_count, rank_width, column_count)
    applied = jnp.einsum("brl,brc->blc", out_basis, placed, preferred_element_type=jnp.float32)
    return applied.astype(BF16).reshape(box_count * leaf_rows, column_count)


def product(matrix, rows):
    return jnp.dot(matrix, rows, preferred_element_type=jnp.float32).astype(BF16)


def stacked(first, second):
    return jnp.concatenate([first, second], axis=0)


def own_half():
    return lax.axis_index("bfly") // 4


def own_place():
    return lax.axis_index("bfly") % 4


def first_box(place):
    return (place % 2) * 4 + (place // 2) * 2


def level_rows(trans_ref, rank, i4, place, i0, level, count):
    return trans_ref.at[i4, :, place % 2, place // 2, i0, pl.ds(level * rank, count * rank)]


def start_all(pairs, sem):
    copies = [pltpu.make_async_copy(source, target, sem) for source, target in pairs]
    for copy in copies:
        copy.start()
    return copies


BOTH = pl.ds(0, 2)


def last_level(rank, trans_ref, i4, r, side, rows_ref):
    slots = rows_ref.reshape(2, rank, trans_ref.shape[-1])
    return level_rows(trans_ref, rank, i4, own_place() ^ r, own_half() ^ side, 8, 1), slots


def spot_tile(target, i4, r, columns):
    row = lax.broadcasted_iota(jnp.int32, (TILE, columns), 0)
    base = i4 * 16 + first_box(own_place() ^ r)
    half = own_half()
    spots = [target[base + (half ^ side) + i3 * 8] % 32 for side in range(2) for i3 in range(2)]
    upper = jnp.where(row == 2, spots[2], spots[3])
    tile = jnp.where(row < 2, jnp.where(row == 0, spots[0], spots[1]), upper)
    return tile.astype(jnp.float32).astype(BF16)


def pack_kernel(rank, target_ref, trans_ref, *refs):
    out_refs, (target, sem, target_sem) = refs[:3], refs[3:]
    group, columns = lax.axis_index("groups"), trans_ref.shape[-1]
    target_copy = pltpu.make_async_copy(target_ref, target, target_sem)
    target_copy.start()
    pairs = []
    for r in (3, 2, 1):
        ref = out_refs[r - 1]
        slots = ref.at[pl.ds(0, 8 * rank)].reshape(2, 2, 2 * rank, columns)
        pairs.append((level_rows(trans_ref, rank, group, own_place() ^ r, BOTH, 6, 2), slots))
        for side in range(2):
            rows = ref.at[pl.ds((8 + 2 * side) * rank, 2 * rank)]
            pairs.append(last_level(rank, trans_ref, group, r, side, rows))
    copies = start_all(pairs, sem)
    target_copy.wait()
    for r in (3, 2, 1):
        out_refs[r - 1][pl.ds(12 * rank, TILE), :] = spot_tile(target, group, r, columns)
    for copy in copies:
        copy.wait()


def gather_kernel(rank, near1, near2, near3, pair_ref, stay_ref):
    for index, ref in enumerate((near1, near2, near3)):
        pair_ref[index] = ref[pl.ds(0, 8 * rank), :]
        stay_ref[index, pl.ds(0, 2 * rank), :] = ref[pl.ds(8 * rank, 2 * rank), :]
        stay_ref[index, pl.ds(2 * rank, TILE), :] = ref[pl.ds(12 * rank, TILE), :]


def late_kernel(rank, late_ref, near1, near2, near3, out_ref):
    tile = []
    for r, (ref, at) in enumerate(((late_ref, 0), (near1, 10), (near2, 10), (near3, 10))):
        out_ref[pl.ds(2 * r * rank, 2 * rank), :] = ref[pl.ds(at * rank, 2 * rank), :]
        tile.append(ref[pl.ds((at + 2) * rank, TILE), :].astype(jnp.float32)[2:4])
    pad = jnp.zeros((TILE - 8, out_ref.shape[-1]), jnp.float32)
    out_ref[pl.ds(8 * rank, TILE), :] = jnp.concatenate([*tile, pad], axis=0).astype(BF16)


def local_kernel(
    levels, rs_ref, leaf_ref, trans_ref, grid_ref, target_ref, out_ref, next_ref, pair_ref, stay_ref, late_ref,
    rs, leaf, trans, ping, pong, target_smem, sem, trans_sem, rest_sem, target_sem
):
    rank = leaf_ref.shape[1]
    target_copy = pltpu.make_async_copy(target_ref, target_smem, target_sem)
    target_copy.start()
    boxes = leaf_ref.shape[0]
    step = boxes // 4
    loads = []
    for part in range(4):
        rows = pl.ds(part * step, step)
        loads.append(
            (
                pltpu.make_async_copy(rs_ref.at[rows], rs.at[rows], sem.at[part, 0]),
                pltpu.make_async_copy(leaf_ref.at[rows], leaf.at[rows], sem.at[part, 1]),
            )
        )
    level_loads = [
        pltpu.make_async_copy(trans_ref.at[:, level], trans.at[level], trans_sem.at[level])
        for level in range(levels)
    ]
    level_loads.append(
        pltpu.make_async_copy(trans_ref.at[:, levels], next_ref, trans_sem.at[levels])
    )
    for pair in loads:
        for copy in pair:
            copy.start()
    for copy in level_loads:
        copy.start()
    group, columns = lax.axis_index("groups"), grid_ref.shape[-1]
    rest = [(level_rows(grid_ref, rank, BOTH, own_place(), BOTH, 6, 2), pair_ref)]
    two = pl.ds(0, 2 * rank)
    rest += [last_level(rank, grid_ref, i4, 0, 0, stay_ref.at[i4, two]) for i4 in range(2)]
    rest.append(last_level(rank, grid_ref, group, 0, 1, late_ref.at[two]))
    rest = start_all(rest, rest_sem)
    target_copy.wait()
    tile = pl.ds(2 * rank, TILE)
    for i4 in range(2):
        stay_ref[i4, tile, :] = spot_tile(target_smem, i4, 0, columns)
    late_ref[tile, :] = spot_tile(target_smem, group, 0, columns)
    for part in range(4):
        for copy in loads[part]:
            copy.wait()
        for box in range(part * step, (part + 1) * step):
            ping[box] = product(leaf[box], rs[box])
    source, target = ping, pong
    for level in range(levels):
        level_loads[level].wait()
        if level == levels - 1:
            target = out_ref
        for box in range(boxes):
            rows = stacked(source[box], source[box ^ (1 << level)])
            target[box] = product(trans[level, box], rows)
        source, target = target, source
    level_loads[levels].wait()
    for copy in rest:
        copy.wait()


def chip_kernel(own_ref, other_ref, trans_ref, *out_refs):
    own = own_place()
    for r in (1, 2, 3, 0):
        base = first_box(own ^ r)
        for q in range(4):
            for i0 in range(2):
                box = base + q * 8 + i0
                rows = stacked(own_ref[box], other_ref[box])
                out_refs[r][q, i0] = product(trans_ref[box], rows)


def quad_kernel(
    rank, box0, box1, box2, box3, pair_ref, near1, near2, near3, far_ref, keep_ref, send_ref, middle
):
    boxes = (box0, box1, box2, box3)
    half, group = own_half(), lax.axis_index("groups")

    def matrix(r, h, i3, i0, level):
        if r == 0:
            return pair_ref[group ^ h, i3, i0, pl.ds(level * rank, rank)]
        ref = far_ref.at[r - 1] if h else (near1, near2, near3)[r - 1]
        start = pl.multiple_of(((i3 * 2 + i0) * 2 + level) * rank, TILE)
        return ref[pl.ds(start, rank), :]

    order = [(r, h, i3) for r in range(4) for h in range(2) for i3 in range(2)]
    for r, h, i3 in order:
        q = (group ^ h) * 2 + i3
        for i0 in range(2):
            rows = stacked(boxes[r][q, i0], boxes[r ^ 1][q, i0])
            middle[r, q, i0] = product(matrix(r, h, i3, i0, 0), rows)
    for out_ref, bit in ((send_ref, 1 - half), (keep_ref, half)):
        for r, h, i3 in order:
            q = (group ^ h) * 2 + i3
            rows = stacked(middle[r, q, bit], middle[r ^ 2, q, bit])
            out_ref[r, q] = product(matrix(r, h, i3, bit, 1), rows)


def last_matrices(rank, bit, stay_ref, near1, near2, near3, far_ref, here_ref, cross_ref):
    group = lax.axis_index("groups")

    def source(side, r, h):
        if side:
            return (here_ref, cross_ref)[h], 2 * r * rank, 8 * rank, 2 * r
        if r == 0:
            return stay_ref.at[group ^ h], 0, 2 * rank, 0
        if h:
            return far_ref.at[r - 1], 0, 2 * rank, 0
        return (near1, near2, near3)[r - 1], 8 * rank, 12 * rank, 0

    boxes = []
    for side in range(2):
        for r in range(4):
            for h in range(2):
                ref, base, tile, row = source(side, r, h)
                spots = ref[pl.ds(tile, TILE), :].astype(jnp.float32)[row : row + 2]
                matrix = ref[pl.ds(pl.multiple_of(base + bit * rank, TILE), rank), :]
                boxes.append((side, r, h, matrix, jnp.where(bit == 0, spots[0:1], spots[1:2])))
    return boxes


def both_halves(side, r, q, keep_ref, recv_ref):
    sides = (keep_ref[r, q], recv_ref[r, q])
    return stacked(sides[side], sides[1 - side])


def send_kernel(rank, keep_ref, recv_ref, *refs):
    group, bit = lax.axis_index("groups"), 1 - lax.axis_index("rhs")
    out_ref, tile = refs[-1], []
    for index, (side, r, h, matrix, spot) in enumerate(last_matrices(rank, bit, *refs[:-1])):
        rows = both_halves(side, r, (group ^ h) * 2 + bit, keep_ref, recv_ref)
        out_ref[pl.ds(index * rank, rank), :] = product(matrix, rows)
        tile.append(spot)
    out_ref[pl.ds(16 * rank, TILE), :] = jnp.concatenate(tile, axis=0).astype(BF16)


def write_rows(box, spot, slot, basis_ref, result, out_ref, sem):
    result[slot] = lax.dot_general(
        basis_ref[spot], box, (((0,), (0,)), ((), ())), preferred_element_type=jnp.float32
    ).astype(BF16)
    copy = pltpu.make_async_copy(result.at[slot], out_ref.at[spot], sem)
    copy.start()
    return copy


def own_kernel(rank, keep_ref, recv_ref, *refs):
    *matrix_refs, basis_ref, out_ref, result, sem, final = refs
    group, bit = lax.axis_index("groups"), lax.axis_index("rhs")
    copies = []
    boxes = last_matrices(rank, bit, *matrix_refs)
    spots = [jnp.max(spot).astype(jnp.int32) for *_, spot in boxes]
    for slot, (side, r, h, matrix, _) in enumerate(boxes):
        rows = both_halves(side, r, (group ^ h) * 2 + bit, keep_ref, recv_ref)
        final[slot] = product(matrix, rows)
    for slot, spot in enumerate(spots):
        copies.append(write_rows(final[slot], spot, slot, basis_ref, result, out_ref, sem))
    for copy in copies:
        copy.wait()


def output_kernel(rank, box_ref, basis_ref, *refs):
    out_ref, result, sem = refs[-3:]
    tile = box_ref[pl.ds(16 * rank, TILE), :].astype(jnp.float32)
    spots = [jnp.max(tile[slot : slot + 1]).astype(jnp.int32) for slot in range(16)]
    copies = []
    for slot in range(16):
        box = box_ref[pl.ds(slot * rank, rank), :]
        copies.append(write_rows(box, spots[slot], slot, basis_ref, result, out_ref, sem))
    for copy in copies:
        copy.wait()


def call(kernel, out_shapes, in_spaces, out_spaces, scratch, flops, moved, aliases=None):
    run = pl.pallas_call(
        kernel,
        out_shape=out_shapes,
        in_specs=[pl.BlockSpec(memory_space=space) for space in in_spaces],
        out_specs=jax.tree.map(lambda space: pl.BlockSpec(memory_space=space), out_spaces),
        scratch_shapes=scratch,
        input_output_aliases=aliases or {},
        compiler_params=pltpu.CompilerParams(vmem_limit_bytes=VMEM_LIMIT),
        cost_estimate=pl.CostEstimate(flops=flops, bytes_accessed=moved, transcendentals=0),
    )

    def placed(*operands):
        return run(
            *(
                pltpu.with_memory_space_constraint(operand, space) if space == pltpu.HBM else operand
                for operand, space in zip(operands, in_spaces)
            )
        )

    return placed


def shape(*dims):
    return jax.ShapeDtypeStruct(dims, BF16)


def bind(kernel, *values):
    return lambda *refs: kernel(*values, *refs)


def move_early(right_sides, leaf_basis, translations, node_target, out_basis):
    boxes, rank, leaf_rows = leaf_basis.shape
    columns = right_sides.shape[1]
    local_levels = boxes.bit_length() - 1
    width = 2 * rank
    block = 2 * rank * columns * 2
    hbm, vmem, smem, dma = pltpu.HBM, pltpu.VMEM, pltpu.SMEM, pltpu.SemaphoreType.DMA
    def across(value, mask):
        return lax.ppermute(value, AXES, [(s, s ^ mask) for s in range(16)])

    def swapped(value):
        return lax.ppermute(value, "groups", [(0, 1), (1, 0)])

    grid = translations.reshape(2, 2, 2, 2, 2, -1, width)
    part = shape(2 * rank + TILE, width)
    near_part = shape(12 * rank + TILE, width)
    near = call(
        bind(pack_kernel, rank),
        (near_part,) * 3,
        (hbm, hbm),
        (vmem,) * 3,
        [smem((boxes,), jnp.int32), dma, dma],
        0,
        2**20,
    )(node_target, grid)
    right_sides, near = lax.optimization_barrier((right_sides, near))
    near = [across(near[r - 1], 2 * r) for r in (1, 2, 3)]
    coefficients, chip_translations, own_pair, stay, late = call(
        bind(local_kernel, local_levels),
        (
            shape(boxes, rank, columns),
            shape(boxes, rank, width),
            shape(2, 2, 2, 2 * rank, width),
            shape(2, *part.shape),
            part,
        ),
        (hbm,) * 5,
        (vmem,) * 5,
        [
            vmem((boxes, leaf_rows, columns), BF16),
            vmem((boxes, rank, leaf_rows), BF16),
            vmem((local_levels, boxes, rank, width), BF16),
            vmem((boxes, rank, columns), BF16),
            vmem((boxes, rank, columns), BF16),
            smem((boxes,), jnp.int32),
            dma((4, 2)),
            dma((local_levels + 1,)),
            dma,
            dma,
        ],
        boxes * rank * columns * 2 * (leaf_rows + local_levels * width),
        6 * 2**20,
    )(
        right_sides.reshape(boxes, leaf_rows, columns), leaf_basis, translations, grid, node_target
    )
    coefficients, near = lax.optimization_barrier((coefficients, near))
    partner = across(coefficients, 1)
    far, far_stay = call(
        bind(gather_kernel, rank),
        (shape(3, 8 * rank, width), shape(3, *part.shape)),
        (vmem,) * 3,
        (vmem,) * 2,
        [],
        0,
        2**20,
    )(*near)
    partner, _ = lax.optimization_barrier((partner, far))
    far = swapped(far)
    slots = call(
        chip_kernel,
        (shape(4, 2, rank, columns),) * 4,
        (vmem,) * 3,
        (vmem,) * 4,
        [],
        boxes * block * width,
        2**21,
    )(coefficients, partner, chip_translations)
    slots = [slots[0]] + [across(slots[r], 2 * r) for r in (1, 2, 3)]
    _, late = lax.optimization_barrier((slots[1], late))
    far_stay = swapped(far_stay)
    here = call(
        bind(late_kernel, rank), shape(8 * rank + TILE, width), (vmem,) * 4, vmem, [], 0, 2**20
    )(late, *near)
    here = across(here, 8)
    keep, send = call(
        bind(quad_kernel, rank),
        (shape(4, 4, rank, columns), shape(4, 4, rank, columns)),
        (vmem,) * 9,
        (vmem,) * 2,
        [vmem((4, 4, 2, rank, columns), BF16)],
        2 * boxes * block * width,
        2**21,
    )(*slots, own_pair, *near, far)
    received = across(send, 8)
    here, _ = lax.optimization_barrier((here, send))
    cross = swapped(here)
    basis = out_basis
    matrices = (stay, *near, far_stay, here, cross)
    send = call(
        bind(send_kernel, rank),
        shape(16 * rank + TILE, columns),
        (vmem,) * 9,
        vmem,
        [],
        boxes * block * width // 2,
        2**20,
    )(keep, received, *matrices)
    partner = across(send, 1)
    rows = shape(boxes, leaf_rows, columns)
    scratch = [vmem((16, leaf_rows, columns), BF16), dma]
    applied = call(
        bind(own_kernel, rank),
        rows,
        (vmem,) * 10,
        hbm,
        [*scratch, vmem((16, rank, columns), BF16)],
        boxes * block * width,
        2**21,
    )(keep, received, *matrices, basis)
    applied = call(
        bind(output_kernel, rank),
        rows,
        (vmem, vmem, hbm),
        hbm,
        scratch,
        boxes * block * width,
        2**21,
        {2: 0},
    )(partner, basis, applied)
    return applied.reshape(boxes * leaf_rows, columns)


def solution(mesh):
    in_specs = (
        P(("groups", "bfly", "rhs"), None),
        P(("bfly", "rhs"), None, None),
        P(("bfly", "rhs"), None, None, None),
        P(("bfly", "rhs")),
        P(("bfly", "rhs"), None, None),
    )
    out_specs = P(("groups", "bfly", "rhs"), None)

    def per_device(right_sides, leaf_basis, translations, node_target, out_basis):
        devices = lax.axis_size(AXES)
        fits = devices == 16 and lax.axis_size("groups") == 2 and leaf_basis.shape[0] == 32
        apply = move_early if fits else exchange_every_level
        return apply(right_sides, leaf_basis, translations, node_target, out_basis)

    return jax.shard_map(
        per_device, mesh=mesh, in_specs=in_specs, out_specs=out_specs, check_vma=False
    )
```

```python
import jax
import jax.numpy as jnp
from jax import lax
from jax.experimental import pallas as pl
from jax.experimental.pallas import tpu as pltpu
from jax.sharding import PartitionSpec as P

AXES = ("bfly", "rhs")
BF16 = jnp.bfloat16
TILE = 16
VMEM_LIMIT = 12 * 2**20


def from_partner(value, axis, distance):
    mask = 2**distance
    pairs = [(source, source ^ mask) for source in range(lax.axis_size(axis))]
    return lax.ppermute(value, axis, pairs)


def combine(current, partner_part, matrices):
    width = current.shape[1]
    own_term = jnp.einsum(
        "bij,bjc->bic", matrices[:, :, :width], current, preferred_element_type=jnp.float32
    )
    other_term = jnp.einsum(
        "bij,bjc->bic", matrices[:, :, width:], partner_part, preferred_element_type=jnp.float32
    )
    return (own_term + other_term).astype(BF16)


def pack_slots(flat_coefficients, slot_key, capacity, slot_total, target_spot):
    box_count = flat_coefficients.shape[0]
    box_iota = jnp.arange(box_count, dtype=jnp.int32)
    earlier = (slot_key[:, None] == slot_key[None, :]) & (box_iota[None, :] < box_iota[:, None])
    order_within = jnp.sum(earlier.astype(jnp.int32), axis=1)
    slot_of_box = slot_key * capacity + order_within
    selector = jnp.arange(slot_total, dtype=jnp.int32)[:, None] == slot_of_box[None, :]
    outgoing = jnp.dot(
        selector.astype(BF16), flat_coefficients, preferred_element_type=jnp.float32
    ).astype(BF16)
    outgoing_spot = jnp.sum(jnp.where(selector, target_spot[None, :] + 1, 0), axis=1) - 1
    return (outgoing, outgoing_spot)


def exchange_every_level(right_sides, leaf_basis, translations, node_target, out_basis):
    box_count = leaf_basis.shape[0]
    rank_width = leaf_basis.shape[1]
    leaf_rows = leaf_basis.shape[2]
    column_count = right_sides.shape[1]
    point_rows = right_sides.reshape(box_count, leaf_rows, column_count)
    coefficients = jnp.einsum(
        "brl,blc->brc", leaf_basis, point_rows, preferred_element_type=jnp.float32
    ).astype(BF16)
    local_levels = box_count.bit_length() - 1
    for level_index in range(local_levels):
        span = 2**level_index
        blocks = coefficients.reshape(box_count // (2 * span), 2, span, rank_width, column_count)
        partner_part = jnp.flip(blocks, 1).reshape(box_count, rank_width, column_count)
        coefficients = combine(coefficients, partner_part, translations[:, level_index])
    device_count = lax.axis_size(AXES)
    device_levels = device_count.bit_length() - 1
    for section_index in range(device_levels):
        partner_part = from_partner(coefficients, AXES, section_index)
        coefficients = combine(
            coefficients, partner_part, translations[:, local_levels + section_index]
        )
    target_device = node_target // box_count
    target_spot = node_target % box_count
    box_iota = jnp.arange(box_count, dtype=jnp.int32)
    flat_coefficients = coefficients.reshape(box_count, rank_width * column_count)
    capacity = max(1, box_count // device_count)
    slot_total = device_count * capacity
    outgoing, outgoing_spot = pack_slots(
        flat_coefficients, target_device, capacity, slot_total, target_spot
    )
    incoming, incoming_spot = (
        lax.all_to_all(outgoing, AXES, split_axis=0, concat_axis=0, tiled=True),
        lax.all_to_all(outgoing_spot, AXES, split_axis=0, concat_axis=0, tiled=True),
    )
    placement_table = (box_iota[:, None] == incoming_spot[None, :]).astype(BF16)
    placed = jnp.dot(placement_table, incoming, preferred_element_type=jnp.float32).astype(BF16)
    placed = placed.reshape(box_count, rank_width, column_count)
    applied = jnp.einsum("brl,brc->blc", out_basis, placed, preferred_element_type=jnp.float32)
    return applied.astype(BF16).reshape(box_count * leaf_rows, column_count)


def product(matrix, rows):
    return jnp.dot(matrix, rows, preferred_element_type=jnp.float32).astype(BF16)


def stacked(first, second):
    return jnp.concatenate([first, second], axis=0)


def own_half():
    return lax.axis_index("bfly") // 4


def own_place():
    return lax.axis_index("bfly") % 4


def first_box(place):
    return (place % 2) * 4 + (place // 2) * 2


def level_rows(trans_ref, rank, i4, place, i0, level, count):
    return trans_ref.at[i4, :, place % 2, place // 2, i0, pl.ds(level * rank, count * rank)]


def start_all(pairs, sem):
    copies = [pltpu.make_async_copy(source, target, sem) for source, target in pairs]
    for copy in copies:
        copy.start()
    return copies


BOTH = pl.ds(0, 2)


def last_level(rank, trans_ref, i4, r, side, rows_ref):
    slots = rows_ref.reshape(2, rank, trans_ref.shape[-1])
    return level_rows(trans_ref, rank, i4, own_place() ^ r, own_half() ^ side, 8, 1), slots


def spot_tile(target, boxes, columns):
    row = lax.broadcasted_iota(jnp.int32, (TILE, columns), 0)
    tile = target[boxes[-1]] % 32
    for index, box in enumerate(boxes[:-1]):
        tile = jnp.where(row == index, target[box] % 32, tile)
    return tile.astype(jnp.float32).astype(BF16)


def late_tile(target, i4, r, columns):
    base = i4 * 16 + first_box(own_place() ^ r) + 1 - own_half()
    return spot_tile(target, (base, base + 8), columns)


def pack_kernel(rank, target_ref, trans_ref, *refs):
    out_refs, (target, sem, target_sem) = refs[:3], refs[3:]
    group, columns = lax.axis_index("groups"), trans_ref.shape[-1]
    target_copy = pltpu.make_async_copy(target_ref, target, target_sem)
    target_copy.start()
    pairs = []
    for r in (3, 2, 1):
        ref = out_refs[r - 1]
        slots = ref.at[pl.ds(0, 8 * rank)].reshape(2, 2, 2 * rank, columns)
        pairs.append((level_rows(trans_ref, rank, group, own_place() ^ r, BOTH, 6, 2), slots))
        pairs.append(last_level(rank, trans_ref, group, r, 1, ref.at[pl.ds(8 * rank, 2 * rank)]))
    copies = start_all(pairs, sem)
    target_copy.wait()
    for r in (3, 2, 1):
        out_refs[r - 1][pl.ds(10 * rank, TILE), :] = late_tile(target, group, r, columns)
    for copy in copies:
        copy.wait()


def gather_kernel(rank, near1, near2, near3, out_ref):
    for index, ref in enumerate((near1, near2, near3)):
        out_ref[index] = ref[pl.ds(0, 8 * rank), :]


def late_kernel(rank, late_ref, near1, near2, near3, out_ref):
    tile = []
    for r, (ref, at) in enumerate(((late_ref, 0), (near1, 8), (near2, 8), (near3, 8))):
        out_ref[pl.ds(2 * r * rank, 2 * rank), :] = ref[pl.ds(at * rank, 2 * rank), :]
        tile.append(ref[pl.ds((at + 2) * rank, TILE), :].astype(jnp.float32)[0:2])
    pad = jnp.zeros((TILE - 8, out_ref.shape[-1]), jnp.float32)
    out_ref[pl.ds(8 * rank, TILE), :] = jnp.concatenate([*tile, pad], axis=0).astype(BF16)


def local_kernel(
    levels, rs_ref, leaf_ref, trans_ref, grid_ref, target_ref, out_ref, next_ref, pair_ref, stay0, stay1, stay2, stay3, late_ref,
    rs, leaf, trans, ping, pong, target_smem, sem, trans_sem, rest_sem, target_sem
):
    rank = leaf_ref.shape[1]
    target_copy = pltpu.make_async_copy(target_ref, target_smem, target_sem)
    target_copy.start()
    boxes = leaf_ref.shape[0]
    step = boxes // 4
    loads = []
    for part in range(4):
        rows = pl.ds(part * step, step)
        loads.append(
            (
                pltpu.make_async_copy(rs_ref.at[rows], rs.at[rows], sem.at[part, 0]),
                pltpu.make_async_copy(leaf_ref.at[rows], leaf.at[rows], sem.at[part, 1]),
            )
        )
    level_loads = [
        pltpu.make_async_copy(trans_ref.at[:, level], trans.at[level], trans_sem.at[level])
        for level in range(levels)
    ]
    level_loads.append(
        pltpu.make_async_copy(trans_ref.at[:, levels], next_ref, trans_sem.at[levels])
    )
    for pair in loads:
        for copy in pair:
            copy.start()
    for copy in level_loads:
        copy.start()
    group, columns = lax.axis_index("groups"), grid_ref.shape[-1]
    rest = [(level_rows(grid_ref, rank, BOTH, own_place(), BOTH, 6, 2), pair_ref)]
    two = pl.ds(0, 2 * rank)
    stay_refs = (stay0, stay1, stay2, stay3)
    for r, ref in enumerate(stay_refs):
        for i4 in range(2):
            rows = ref.at[pl.ds(2 * i4 * rank, 2 * rank)]
            rest.append(last_level(rank, grid_ref, i4, r, 0, rows))
    rest.append(last_level(rank, grid_ref, group, 0, 1, late_ref.at[two]))
    rest = start_all(rest, rest_sem)
    target_copy.wait()
    for r, ref in enumerate(stay_refs):
        base = first_box(own_place() ^ r) + own_half()
        spots = [base + q * 8 for q in range(4)]
        ref[pl.ds(4 * rank, TILE), :] = spot_tile(target_smem, spots, columns)
    late_ref[pl.ds(2 * rank, TILE), :] = late_tile(target_smem, group, 0, columns)
    for part in range(4):
        for copy in loads[part]:
            copy.wait()
        for box in range(part * step, (part + 1) * step):
            ping[box] = product(leaf[box], rs[box])
    source, target = ping, pong
    for level in range(levels):
        level_loads[level].wait()
        if level == levels - 1:
            target = out_ref
        for box in range(boxes):
            rows = stacked(source[box], source[box ^ (1 << level)])
            target[box] = product(trans[level, box], rows)
        source, target = target, source
    level_loads[levels].wait()
    for copy in rest:
        copy.wait()


def chip_kernel(own_ref, other_ref, trans_ref, *out_refs):
    own = own_place()
    for r in (1, 2, 3, 0):
        base = first_box(own ^ r)
        for q in range(4):
            for i0 in range(2):
                box = base + q * 8 + i0
                rows = stacked(own_ref[box], other_ref[box])
                out_refs[r][q, i0] = product(trans_ref[box], rows)


def quad_kernel(
    rank, box0, box1, box2, box3, pair_ref, near1, near2, near3, far_ref, keep_ref, send_ref, middle
):
    boxes = (box0, box1, box2, box3)
    half, group = own_half(), lax.axis_index("groups")

    def matrix(r, h, i3, i0, level):
        if r == 0:
            return pair_ref[group ^ h, i3, i0, pl.ds(level * rank, rank)]
        ref = far_ref.at[r - 1] if h else (near1, near2, near3)[r - 1]
        start = pl.multiple_of(((i3 * 2 + i0) * 2 + level) * rank, TILE)
        return ref[pl.ds(start, rank), :]

    order = [(r, h, i3) for r in range(4) for h in range(2) for i3 in range(2)]
    for r, h, i3 in order:
        q = (group ^ h) * 2 + i3
        for i0 in range(2):
            rows = stacked(boxes[r][q, i0], boxes[r ^ 1][q, i0])
            middle[r, q, i0] = product(matrix(r, h, i3, i0, 0), rows)
    for out_ref, bit in ((send_ref, 1 - half), (keep_ref, half)):
        for r, h, i3 in order:
            q = (group ^ h) * 2 + i3
            rows = stacked(middle[r, q, bit], middle[r ^ 2, q, bit])
            out_ref[r, q] = product(matrix(r, h, i3, bit, 1), rows)


def last_matrices(rank, bit, stay0, stay1, stay2, stay3, here_ref, cross_ref):
    group = lax.axis_index("groups")

    def source(side, r, h):
        if side:
            return (here_ref, cross_ref)[h], 2 * r, 8 * rank, 2 * r, 2 * r
        i4 = group ^ h
        return (stay0, stay1, stay2, stay3)[r], 2 * i4, 4 * rank, i4, None

    boxes = []
    for side in range(2):
        for r in range(4):
            for h in range(2):
                ref, first, tile, i4, row = source(side, r, h)
                spots = ref[pl.ds(tile, TILE), :].astype(jnp.float32)
                spots = jnp.where(i4 == 0, spots[0:2], spots[2:4]) if row is None else spots[row : row + 2]
                matrix = ref[pl.ds(pl.multiple_of((first + bit) * rank, TILE), rank), :]
                boxes.append((side, r, h, matrix, jnp.where(bit == 0, spots[0:1], spots[1:2])))
    return boxes


def both_halves(side, r, q, keep_ref, recv_ref):
    sides = (keep_ref[r, q], recv_ref[r, q])
    return stacked(sides[side], sides[1 - side])


def send_kernel(rank, keep_ref, recv_ref, *refs):
    group, bit = lax.axis_index("groups"), 1 - lax.axis_index("rhs")
    out_ref, tile = refs[-1], []
    for index, (side, r, h, matrix, spot) in enumerate(last_matrices(rank, bit, *refs[:-1])):
        rows = both_halves(side, r, (group ^ h) * 2 + bit, keep_ref, recv_ref)
        out_ref[pl.ds(index * rank, rank), :] = product(matrix, rows)
        tile.append(spot)
    out_ref[pl.ds(16 * rank, TILE), :] = jnp.concatenate(tile, axis=0).astype(BF16)


def write_rows(box, spot, slot, basis_ref, result, out_ref, sem):
    result[slot] = lax.dot_general(
        basis_ref[spot], box, (((0,), (0,)), ((), ())), preferred_element_type=jnp.float32
    ).astype(BF16)
    copy = pltpu.make_async_copy(result.at[slot], out_ref.at[spot], sem)
    copy.start()
    return copy


def own_kernel(rank, keep_ref, recv_ref, *refs):
    *matrix_refs, basis_ref, out_ref, result, sem, final = refs
    group, bit = lax.axis_index("groups"), lax.axis_index("rhs")
    copies = []
    boxes = last_matrices(rank, bit, *matrix_refs)
    spots = [jnp.max(spot).astype(jnp.int32) for *_, spot in boxes]
    for slot, (side, r, h, matrix, _) in enumerate(boxes):
        rows = both_halves(side, r, (group ^ h) * 2 + bit, keep_ref, recv_ref)
        final[slot] = product(matrix, rows)
    for slot, spot in enumerate(spots):
        copies.append(write_rows(final[slot], spot, slot, basis_ref, result, out_ref, sem))
    for copy in copies:
        copy.wait()


def output_kernel(rank, box_ref, basis_ref, *refs):
    out_ref, result, sem = refs[-3:]
    tile = box_ref[pl.ds(16 * rank, TILE), :].astype(jnp.float32)
    spots = [jnp.max(tile[slot : slot + 1]).astype(jnp.int32) for slot in range(16)]
    copies = []
    for slot in range(16):
        box = box_ref[pl.ds(slot * rank, rank), :]
        copies.append(write_rows(box, spots[slot], slot, basis_ref, result, out_ref, sem))
    for copy in copies:
        copy.wait()


def call(kernel, out_shapes, in_spaces, out_spaces, scratch, flops, moved, aliases=None):
    run = pl.pallas_call(
        kernel,
        out_shape=out_shapes,
        in_specs=[pl.BlockSpec(memory_space=space) for space in in_spaces],
        out_specs=jax.tree.map(lambda space: pl.BlockSpec(memory_space=space), out_spaces),
        scratch_shapes=scratch,
        input_output_aliases=aliases or {},
        compiler_params=pltpu.CompilerParams(vmem_limit_bytes=VMEM_LIMIT),
        cost_estimate=pl.CostEstimate(flops=flops, bytes_accessed=moved, transcendentals=0),
    )

    def placed(*operands):
        return run(
            *(
                pltpu.with_memory_space_constraint(operand, space) if space == pltpu.HBM else operand
                for operand, space in zip(operands, in_spaces)
            )
        )

    return placed


def shape(*dims):
    return jax.ShapeDtypeStruct(dims, BF16)


def bind(kernel, *values):
    return lambda *refs: kernel(*values, *refs)


def move_early(right_sides, leaf_basis, translations, node_target, out_basis):
    boxes, rank, leaf_rows = leaf_basis.shape
    columns = right_sides.shape[1]
    local_levels = boxes.bit_length() - 1
    width = 2 * rank
    block = 2 * rank * columns * 2
    hbm, vmem, smem, dma = pltpu.HBM, pltpu.VMEM, pltpu.SMEM, pltpu.SemaphoreType.DMA
    def across(value, mask):
        return lax.ppermute(value, AXES, [(s, s ^ mask) for s in range(16)])

    def swapped(value):
        return lax.ppermute(value, "groups", [(0, 1), (1, 0)])

    grid = translations.reshape(2, 2, 2, 2, 2, -1, width)
    part = shape(2 * rank + TILE, width)
    near_part = shape(10 * rank + TILE, width)
    stay_part = shape(4 * rank + TILE, width)
    near = call(
        bind(pack_kernel, rank),
        (near_part,) * 3,
        (hbm, hbm),
        (vmem,) * 3,
        [smem((boxes,), jnp.int32), dma, dma],
        0,
        2**20,
    )(node_target, grid)
    right_sides, near = lax.optimization_barrier((right_sides, near))
    near = [across(near[r - 1], 2 * r) for r in (1, 2, 3)]
    coefficients, chip_translations, own_pair, *stay, late = call(
        bind(local_kernel, local_levels),
        (
            shape(boxes, rank, columns),
            shape(boxes, rank, width),
            shape(2, 2, 2, 2 * rank, width),
        )
        + (stay_part,) * 4
        + (part,),
        (hbm,) * 5,
        (vmem,) * 8,
        [
            vmem((boxes, leaf_rows, columns), BF16),
            vmem((boxes, rank, leaf_rows), BF16),
            vmem((local_levels, boxes, rank, width), BF16),
            vmem((boxes, rank, columns), BF16),
            vmem((boxes, rank, columns), BF16),
            smem((boxes,), jnp.int32),
            dma((4, 2)),
            dma((local_levels + 1,)),
            dma,
            dma,
        ],
        boxes * rank * columns * 2 * (leaf_rows + local_levels * width),
        6 * 2**20,
    )(
        right_sides.reshape(boxes, leaf_rows, columns), leaf_basis, translations, grid, node_target
    )
    coefficients, near = lax.optimization_barrier((coefficients, near))
    partner = across(coefficients, 1)
    far = call(bind(gather_kernel, rank), shape(3, 8 * rank, width), (vmem,) * 3, vmem, [], 0, 2**20)(*near)
    partner, _ = lax.optimization_barrier((partner, far))
    far = swapped(far)
    slots = call(
        chip_kernel,
        (shape(4, 2, rank, columns),) * 4,
        (vmem,) * 3,
        (vmem,) * 4,
        [],
        boxes * block * width,
        2**21,
    )(coefficients, partner, chip_translations)
    slots = [slots[0]] + [across(slots[r], 2 * r) for r in (1, 2, 3)]
    _, late = lax.optimization_barrier((slots[1], late))
    here = call(
        bind(late_kernel, rank), shape(8 * rank + TILE, width), (vmem,) * 4, vmem, [], 0, 2**20
    )(late, *near)
    here = across(here, 8)
    keep, send = call(
        bind(quad_kernel, rank),
        (shape(4, 4, rank, columns), shape(4, 4, rank, columns)),
        (vmem,) * 9,
        (vmem,) * 2,
        [vmem((4, 4, 2, rank, columns), BF16)],
        2 * boxes * block * width,
        2**21,
    )(*slots, own_pair, *near, far)
    received = across(send, 8)
    stay, _ = lax.optimization_barrier((stay, send))
    stay = [stay[0]] + [across(stay[r], 2 * r) for r in (1, 2, 3)]
    here, stay[1], stay[2], stay[3] = lax.optimization_barrier((here, stay[1], stay[2], stay[3]))
    cross = swapped(here)
    basis = out_basis
    matrices = (*stay, here, cross)
    send = call(
        bind(send_kernel, rank),
        shape(16 * rank + TILE, columns),
        (vmem,) * 8,
        vmem,
        [],
        boxes * block * width // 2,
        2**20,
    )(keep, received, *matrices)
    partner = across(send, 1)
    rows = shape(boxes, leaf_rows, columns)
    scratch = [vmem((16, leaf_rows, columns), BF16), dma]
    applied = call(
        bind(own_kernel, rank),
        rows,
        (vmem,) * 9,
        hbm,
        [*scratch, vmem((16, rank, columns), BF16)],
        boxes * block * width,
        2**21,
    )(keep, received, *matrices, basis)
    applied = call(
        bind(output_kernel, rank),
        rows,
        (vmem, vmem, hbm),
        hbm,
        scratch,
        boxes * block * width,
        2**21,
        {2: 0},
    )(partner, basis, applied)
    return applied.reshape(boxes * leaf_rows, columns)


def solution(mesh):
    in_specs = (
        P(("groups", "bfly", "rhs"), None),
        P(("bfly", "rhs"), None, None),
        P(("bfly", "rhs"), None, None, None),
        P(("bfly", "rhs")),
        P(("bfly", "rhs"), None, None),
    )
    out_specs = P(("groups", "bfly", "rhs"), None)

    def per_device(right_sides, leaf_basis, translations, node_target, out_basis):
        devices = lax.axis_size(AXES)
        fits = devices == 16 and lax.axis_size("groups") == 2 and leaf_basis.shape[0] == 32
        apply = move_early if fits else exchange_every_level
        return apply(right_sides, leaf_basis, translations, node_target, out_basis)

    return jax.shard_map(
        per_device, mesh=mesh, in_specs=in_specs, out_specs=out_specs, check_vma=False
    )
```

```python
import jax
import jax.numpy as jnp
from jax import lax
from jax.experimental import pallas as pl
from jax.experimental.pallas import tpu as pltpu
from jax.sharding import PartitionSpec as P

AXES = ("bfly", "rhs")
BF16 = jnp.bfloat16
TILE = 16
VMEM_LIMIT = 12 * 2**20


def from_partner(value, axis, distance):
    mask = 2**distance
    pairs = [(source, source ^ mask) for source in range(lax.axis_size(axis))]
    return lax.ppermute(value, axis, pairs)


def combine(current, partner_part, matrices):
    width = current.shape[1]
    own_term = jnp.einsum(
        "bij,bjc->bic", matrices[:, :, :width], current, preferred_element_type=jnp.float32
    )
    other_term = jnp.einsum(
        "bij,bjc->bic", matrices[:, :, width:], partner_part, preferred_element_type=jnp.float32
    )
    return (own_term + other_term).astype(BF16)


def pack_slots(flat_coefficients, slot_key, capacity, slot_total, target_spot):
    box_count = flat_coefficients.shape[0]
    box_iota = jnp.arange(box_count, dtype=jnp.int32)
    earlier = (slot_key[:, None] == slot_key[None, :]) & (box_iota[None, :] < box_iota[:, None])
    order_within = jnp.sum(earlier.astype(jnp.int32), axis=1)
    slot_of_box = slot_key * capacity + order_within
    selector = jnp.arange(slot_total, dtype=jnp.int32)[:, None] == slot_of_box[None, :]
    outgoing = jnp.dot(
        selector.astype(BF16), flat_coefficients, preferred_element_type=jnp.float32
    ).astype(BF16)
    outgoing_spot = jnp.sum(jnp.where(selector, target_spot[None, :] + 1, 0), axis=1) - 1
    return (outgoing, outgoing_spot)


def exchange_every_level(right_sides, leaf_basis, translations, node_target, out_basis):
    box_count = leaf_basis.shape[0]
    rank_width = leaf_basis.shape[1]
    leaf_rows = leaf_basis.shape[2]
    column_count = right_sides.shape[1]
    point_rows = right_sides.reshape(box_count, leaf_rows, column_count)
    coefficients = jnp.einsum(
        "brl,blc->brc", leaf_basis, point_rows, preferred_element_type=jnp.float32
    ).astype(BF16)
    local_levels = box_count.bit_length() - 1
    for level_index in range(local_levels):
        span = 2**level_index
        blocks = coefficients.reshape(box_count // (2 * span), 2, span, rank_width, column_count)
        partner_part = jnp.flip(blocks, 1).reshape(box_count, rank_width, column_count)
        coefficients = combine(coefficients, partner_part, translations[:, level_index])
    device_count = lax.axis_size(AXES)
    device_levels = device_count.bit_length() - 1
    for section_index in range(device_levels):
        partner_part = from_partner(coefficients, AXES, section_index)
        coefficients = combine(
            coefficients, partner_part, translations[:, local_levels + section_index]
        )
    target_device = node_target // box_count
    target_spot = node_target % box_count
    box_iota = jnp.arange(box_count, dtype=jnp.int32)
    flat_coefficients = coefficients.reshape(box_count, rank_width * column_count)
    capacity = max(1, box_count // device_count)
    slot_total = device_count * capacity
    outgoing, outgoing_spot = pack_slots(
        flat_coefficients, target_device, capacity, slot_total, target_spot
    )
    incoming, incoming_spot = (
        lax.all_to_all(outgoing, AXES, split_axis=0, concat_axis=0, tiled=True),
        lax.all_to_all(outgoing_spot, AXES, split_axis=0, concat_axis=0, tiled=True),
    )
    placement_table = (box_iota[:, None] == incoming_spot[None, :]).astype(BF16)
    placed = jnp.dot(placement_table, incoming, preferred_element_type=jnp.float32).astype(BF16)
    placed = placed.reshape(box_count, rank_width, column_count)
    applied = jnp.einsum("brl,brc->blc", out_basis, placed, preferred_element_type=jnp.float32)
    return applied.astype(BF16).reshape(box_count * leaf_rows, column_count)


def product(matrix, rows):
    return jnp.dot(matrix, rows, preferred_element_type=jnp.float32).astype(BF16)


def stacked(first, second):
    return jnp.concatenate([first, second], axis=0)


def products(first, second, own, other):
    width = own.shape[0]
    turned = jnp.concatenate([second[:, width:], second[:, :width]], axis=1)
    both = product(stacked(first, turned), stacked(own, other))
    return both[:width], both[width:]


def own_half():
    return lax.axis_index("bfly") // 4


def own_place():
    return lax.axis_index("bfly") % 4


def first_box(place):
    return (place % 2) * 4 + (place // 2) * 2


def level_rows(trans_ref, rank, i4, place, i0, level, count):
    return trans_ref.at[i4, :, place % 2, place // 2, i0, pl.ds(level * rank, count * rank)]


def start_all(pairs, sem):
    copies = [pltpu.make_async_copy(source, target, sem) for source, target in pairs]
    for copy in copies:
        copy.start()
    return copies


BOTH = pl.ds(0, 2)


def last_level(rank, trans_ref, i4, r, side, rows_ref):
    slots = rows_ref.reshape(2, rank, trans_ref.shape[-1])
    return level_rows(trans_ref, rank, i4, own_place() ^ r, own_half() ^ side, 8, 1), slots


def spot_tile(target, boxes, columns):
    row = lax.broadcasted_iota(jnp.int32, (TILE, columns), 0)
    tile = target[boxes[-1]] % 32
    for index, box in enumerate(boxes[:-1]):
        tile = jnp.where(row == index, target[box] % 32, tile)
    return tile.astype(jnp.float32).astype(BF16)


def late_tile(target, i4, r, columns):
    base = i4 * 16 + first_box(own_place() ^ r) + 1 - own_half()
    return spot_tile(target, (base, base + 8), columns)


def pack_kernel(rank, target_ref, trans_ref, *refs):
    out_refs, (target, sem, target_sem) = refs[:3], refs[3:]
    group, columns = lax.axis_index("groups"), trans_ref.shape[-1]
    target_copy = pltpu.make_async_copy(target_ref, target, target_sem)
    target_copy.start()
    pairs = []
    for r in (3, 2, 1):
        ref = out_refs[r - 1]
        slots = ref.at[pl.ds(0, 8 * rank)].reshape(2, 2, 2 * rank, columns)
        pairs.append((level_rows(trans_ref, rank, group, own_place() ^ r, BOTH, 6, 2), slots))
        pairs.append(last_level(rank, trans_ref, group, r, 1, ref.at[pl.ds(8 * rank, 2 * rank)]))
    copies = start_all(pairs, sem)
    target_copy.wait()
    for r in (3, 2, 1):
        out_refs[r - 1][pl.ds(10 * rank, TILE), :] = late_tile(target, group, r, columns)
    for copy in copies:
        copy.wait()


def gather_kernel(rank, near1, near2, near3, out_ref):
    for index, ref in enumerate((near1, near2, near3)):
        out_ref[index] = ref[pl.ds(0, 8 * rank), :]


def late_kernel(rank, late_ref, near1, near2, near3, out_ref):
    tile = []
    for r, (ref, at) in enumerate(((late_ref, 0), (near1, 8), (near2, 8), (near3, 8))):
        out_ref[pl.ds(2 * r * rank, 2 * rank), :] = ref[pl.ds(at * rank, 2 * rank), :]
        tile.append(ref[pl.ds((at + 2) * rank, TILE), :].astype(jnp.float32)[0:2])
    pad = jnp.zeros((TILE - 8, out_ref.shape[-1]), jnp.float32)
    out_ref[pl.ds(8 * rank, TILE), :] = jnp.concatenate([*tile, pad], axis=0).astype(BF16)


def local_kernel(
    levels, rs_ref, leaf_ref, trans_ref, grid_ref, target_ref, out_ref, next_ref, pair_ref, stay0, stay1, stay2, stay3, late_ref,
    rs, leaf, trans, ping, pong, target_smem, sem, trans_sem, rest_sem, target_sem
):
    rank = leaf_ref.shape[1]
    target_copy = pltpu.make_async_copy(target_ref, target_smem, target_sem)
    target_copy.start()
    boxes = leaf_ref.shape[0]
    step = boxes // 4
    loads = []
    for part in range(4):
        rows = pl.ds(part * step, step)
        loads.append(
            (
                pltpu.make_async_copy(rs_ref.at[rows], rs.at[rows], sem.at[part, 0]),
                pltpu.make_async_copy(leaf_ref.at[rows], leaf.at[rows], sem.at[part, 1]),
            )
        )
    level_loads = [
        pltpu.make_async_copy(trans_ref.at[:, level], trans.at[level], trans_sem.at[level])
        for level in range(levels)
    ]
    level_loads.append(
        pltpu.make_async_copy(trans_ref.at[:, levels], next_ref, trans_sem.at[levels])
    )
    for pair in loads:
        for copy in pair:
            copy.start()
    for copy in level_loads:
        copy.start()
    group, columns = lax.axis_index("groups"), grid_ref.shape[-1]
    rest = [(level_rows(grid_ref, rank, BOTH, own_place(), BOTH, 6, 2), pair_ref)]
    two = pl.ds(0, 2 * rank)
    stay_refs = (stay0, stay1, stay2, stay3)
    for r, ref in enumerate(stay_refs):
        for i4 in range(2):
            rows = ref.at[pl.ds(2 * i4 * rank, 2 * rank)]
            rest.append(last_level(rank, grid_ref, i4, r, 0, rows))
    rest.append(last_level(rank, grid_ref, group, 0, 1, late_ref.at[two]))
    rest = start_all(rest, rest_sem)
    target_copy.wait()
    for r, ref in enumerate(stay_refs):
        base = first_box(own_place() ^ r) + own_half()
        spots = [base + q * 8 for q in range(4)]
        ref[pl.ds(4 * rank, TILE), :] = spot_tile(target_smem, spots, columns)
    late_ref[pl.ds(2 * rank, TILE), :] = late_tile(target_smem, group, 0, columns)
    for part in range(4):
        for copy in loads[part]:
            copy.wait()
        for box in range(part * step, (part + 1) * step):
            ping[box] = product(leaf[box], rs[box])
    source, target = ping, pong
    for level in range(levels):
        level_loads[level].wait()
        if level == levels - 1:
            target = out_ref
        for box in range(boxes):
            rows = stacked(source[box], source[box ^ (1 << level)])
            target[box] = product(trans[level, box], rows)
        source, target = target, source
    level_loads[levels].wait()
    for copy in rest:
        copy.wait()


def chip_kernel(own_ref, other_ref, trans_ref, *out_refs):
    own = own_place()
    for r in (1, 2, 3, 0):
        base = first_box(own ^ r)
        for q in range(4):
            for i0 in range(2):
                box = base + q * 8 + i0
                rows = stacked(own_ref[box], other_ref[box])
                out_refs[r][q, i0] = product(trans_ref[box], rows)


def quad_kernel(
    rank, box0, box1, box2, box3, pair_ref, near1, near2, near3, far_ref, keep_ref, send_ref, middle
):
    boxes = (box0, box1, box2, box3)
    half, group = own_half(), lax.axis_index("groups")

    def matrix(r, h, i3, i0, level):
        if r == 0:
            return pair_ref[group ^ h, i3, i0, pl.ds(level * rank, rank)]
        ref = far_ref.at[r - 1] if h else (near1, near2, near3)[r - 1]
        start = pl.multiple_of(((i3 * 2 + i0) * 2 + level) * rank, TILE)
        return ref[pl.ds(start, rank), :]

    slots = [(h, i3) for h in range(2) for i3 in range(2)]
    for r in (0, 2):
        for h, i3 in slots:
            q = (group ^ h) * 2 + i3
            for i0 in range(2):
                pair = matrix(r, h, i3, i0, 0), matrix(r + 1, h, i3, i0, 0)
                both = products(*pair, boxes[r][q, i0], boxes[r + 1][q, i0])
                middle[r, q, i0], middle[r + 1, q, i0] = both
    for out_ref, bit in ((send_ref, 1 - half), (keep_ref, half)):
        for r in (0, 1):
            for h, i3 in slots:
                q = (group ^ h) * 2 + i3
                pair = matrix(r, h, i3, bit, 1), matrix(r + 2, h, i3, bit, 1)
                both = products(*pair, middle[r, q, bit], middle[r + 2, q, bit])
                out_ref[r, q], out_ref[r + 2, q] = both


def last_matrices(rank, bit, stay0, stay1, stay2, stay3, here_ref, cross_ref):
    group = lax.axis_index("groups")

    def source(side, r, h):
        if side:
            return (here_ref, cross_ref)[h], 2 * r, 8 * rank, 2 * r, 2 * r
        i4 = group ^ h
        return (stay0, stay1, stay2, stay3)[r], 2 * i4, 4 * rank, i4, None

    boxes = []
    for side in range(2):
        for r in range(4):
            for h in range(2):
                ref, first, tile, i4, row = source(side, r, h)
                spots = ref[pl.ds(tile, TILE), :].astype(jnp.float32)
                spots = jnp.where(i4 == 0, spots[0:2], spots[2:4]) if row is None else spots[row : row + 2]
                matrix = ref[pl.ds(pl.multiple_of((first + bit) * rank, TILE), rank), :]
                boxes.append((side, r, h, matrix, jnp.where(bit == 0, spots[0:1], spots[1:2])))
    return boxes


def both_halves(side, r, q, keep_ref, recv_ref):
    sides = (keep_ref[r, q], recv_ref[r, q])
    return stacked(sides[side], sides[1 - side])


def send_kernel(rank, keep_ref, recv_ref, *refs):
    group, bit = lax.axis_index("groups"), 1 - lax.axis_index("rhs")
    out_ref, tile = refs[-1], []
    for index, (side, r, h, matrix, spot) in enumerate(last_matrices(rank, bit, *refs[:-1])):
        rows = both_halves(side, r, (group ^ h) * 2 + bit, keep_ref, recv_ref)
        out_ref[pl.ds(index * rank, rank), :] = product(matrix, rows)
        tile.append(spot)
    out_ref[pl.ds(16 * rank, TILE), :] = jnp.concatenate(tile, axis=0).astype(BF16)


def write_rows(box, spot, slot, basis_ref, result, out_ref, sem):
    result[slot] = lax.dot_general(
        basis_ref[spot], box, (((0,), (0,)), ((), ())), preferred_element_type=jnp.float32
    ).astype(BF16)
    copy = pltpu.make_async_copy(result.at[slot], out_ref.at[spot], sem)
    copy.start()
    return copy


def own_kernel(rank, keep_ref, recv_ref, *refs):
    *matrix_refs, basis_ref, out_ref, result, sem, final = refs
    group, bit = lax.axis_index("groups"), lax.axis_index("rhs")
    copies = []
    boxes = last_matrices(rank, bit, *matrix_refs)
    spots = [jnp.max(spot).astype(jnp.int32) for *_, spot in boxes]
    for slot, (side, r, h, matrix, _) in enumerate(boxes):
        rows = both_halves(side, r, (group ^ h) * 2 + bit, keep_ref, recv_ref)
        final[slot] = product(matrix, rows)
    for slot, spot in enumerate(spots):
        copies.append(write_rows(final[slot], spot, slot, basis_ref, result, out_ref, sem))
    for copy in copies:
        copy.wait()


def output_kernel(rank, box_ref, basis_ref, *refs):
    out_ref, result, sem = refs[-3:]
    tile = box_ref[pl.ds(16 * rank, TILE), :].astype(jnp.float32)
    spots = [jnp.max(tile[slot : slot + 1]).astype(jnp.int32) for slot in range(16)]
    copies = []
    for slot in range(16):
        box = box_ref[pl.ds(slot * rank, rank), :]
        copies.append(write_rows(box, spots[slot], slot, basis_ref, result, out_ref, sem))
    for copy in copies:
        copy.wait()


def call(kernel, out_shapes, in_spaces, out_spaces, scratch, flops, moved, aliases=None):
    run = pl.pallas_call(
        kernel,
        out_shape=out_shapes,
        in_specs=[pl.BlockSpec(memory_space=space) for space in in_spaces],
        out_specs=jax.tree.map(lambda space: pl.BlockSpec(memory_space=space), out_spaces),
        scratch_shapes=scratch,
        input_output_aliases=aliases or {},
        compiler_params=pltpu.CompilerParams(vmem_limit_bytes=VMEM_LIMIT),
        cost_estimate=pl.CostEstimate(flops=flops, bytes_accessed=moved, transcendentals=0),
    )

    def placed(*operands):
        return run(
            *(
                pltpu.with_memory_space_constraint(operand, space) if space == pltpu.HBM else operand
                for operand, space in zip(operands, in_spaces)
            )
        )

    return placed


def shape(*dims):
    return jax.ShapeDtypeStruct(dims, BF16)


def bind(kernel, *values):
    return lambda *refs: kernel(*values, *refs)


def move_early(right_sides, leaf_basis, translations, node_target, out_basis):
    boxes, rank, leaf_rows = leaf_basis.shape
    columns = right_sides.shape[1]
    local_levels = boxes.bit_length() - 1
    width = 2 * rank
    block = 2 * rank * columns * 2
    hbm, vmem, smem, dma = pltpu.HBM, pltpu.VMEM, pltpu.SMEM, pltpu.SemaphoreType.DMA
    def across(value, mask):
        return lax.ppermute(value, AXES, [(s, s ^ mask) for s in range(16)])

    def swapped(value):
        return lax.ppermute(value, "groups", [(0, 1), (1, 0)])

    grid = translations.reshape(2, 2, 2, 2, 2, -1, width)
    part = shape(2 * rank + TILE, width)
    near_part = shape(10 * rank + TILE, width)
    stay_part = shape(4 * rank + TILE, width)
    near = call(
        bind(pack_kernel, rank),
        (near_part,) * 3,
        (hbm, hbm),
        (vmem,) * 3,
        [smem((boxes,), jnp.int32), dma, dma],
        0,
        2**20,
    )(node_target, grid)
    right_sides, near = lax.optimization_barrier((right_sides, near))
    near = [across(near[r - 1], 2 * r) for r in (1, 2, 3)]
    coefficients, chip_translations, own_pair, *stay, late = call(
        bind(local_kernel, local_levels),
        (
            shape(boxes, rank, columns),
            shape(boxes, rank, width),
            shape(2, 2, 2, 2 * rank, width),
        )
        + (stay_part,) * 4
        + (part,),
        (hbm,) * 5,
        (vmem,) * 8,
        [
            vmem((boxes, leaf_rows, columns), BF16),
            vmem((boxes, rank, leaf_rows), BF16),
            vmem((local_levels, boxes, rank, width), BF16),
            vmem((boxes, rank, columns), BF16),
            vmem((boxes, rank, columns), BF16),
            smem((boxes,), jnp.int32),
            dma((4, 2)),
            dma((local_levels + 1,)),
            dma,
            dma,
        ],
        boxes * rank * columns * 2 * (leaf_rows + local_levels * width),
        6 * 2**20,
    )(
        right_sides.reshape(boxes, leaf_rows, columns), leaf_basis, translations, grid, node_target
    )
    coefficients, near = lax.optimization_barrier((coefficients, near))
    partner = across(coefficients, 1)
    far = call(bind(gather_kernel, rank), shape(3, 8 * rank, width), (vmem,) * 3, vmem, [], 0, 2**20)(*near)
    partner, _ = lax.optimization_barrier((partner, far))
    far = swapped(far)
    slots = call(
        chip_kernel,
        (shape(4, 2, rank, columns),) * 4,
        (vmem,) * 3,
        (vmem,) * 4,
        [],
        boxes * block * width,
        2**21,
    )(coefficients, partner, chip_translations)
    slots = [slots[0]] + [across(slots[r], 2 * r) for r in (1, 2, 3)]
    _, late = lax.optimization_barrier((slots[1], late))
    here = call(
        bind(late_kernel, rank), shape(8 * rank + TILE, width), (vmem,) * 4, vmem, [], 0, 2**20
    )(late, *near)
    here = across(here, 8)
    keep, send = call(
        bind(quad_kernel, rank),
        (shape(4, 4, rank, columns), shape(4, 4, rank, columns)),
        (vmem,) * 9,
        (vmem,) * 2,
        [vmem((4, 4, 2, rank, columns), BF16)],
        2 * boxes * block * width,
        2**21,
    )(*slots, own_pair, *near, far)
    received = across(send, 8)
    stay, _ = lax.optimization_barrier((stay, send))
    stay = [stay[0]] + [across(stay[r], 2 * r) for r in (1, 2, 3)]
    here, stay[1], stay[2], stay[3] = lax.optimization_barrier((here, stay[1], stay[2], stay[3]))
    cross = swapped(here)
    basis = out_basis
    matrices = (*stay, here, cross)
    send = call(
        bind(send_kernel, rank),
        shape(16 * rank + TILE, columns),
        (vmem,) * 8,
        vmem,
        [],
        boxes * block * width // 2,
        2**20,
    )(keep, received, *matrices)
    partner = across(send, 1)
    rows = shape(boxes, leaf_rows, columns)
    scratch = [vmem((16, leaf_rows, columns), BF16), dma]
    applied = call(
        bind(own_kernel, rank),
        rows,
        (vmem,) * 9,
        hbm,
        [*scratch, vmem((16, rank, columns), BF16)],
        boxes * block * width,
        2**21,
    )(keep, received, *matrices, basis)
    applied = call(
        bind(output_kernel, rank),
        rows,
        (vmem, vmem, hbm),
        hbm,
        scratch,
        boxes * block * width,
        2**21,
        {2: 0},
    )(partner, basis, applied)
    return applied.reshape(boxes * leaf_rows, columns)


def solution(mesh):
    in_specs = (
        P(("groups", "bfly", "rhs"), None),
        P(("bfly", "rhs"), None, None),
        P(("bfly", "rhs"), None, None, None),
        P(("bfly", "rhs")),
        P(("bfly", "rhs"), None, None),
    )
    out_specs = P(("groups", "bfly", "rhs"), None)

    def per_device(right_sides, leaf_basis, translations, node_target, out_basis):
        devices = lax.axis_size(AXES)
        fits = devices == 16 and lax.axis_size("groups") == 2 and leaf_basis.shape[0] == 32
        apply = move_early if fits else exchange_every_level
        return apply(right_sides, leaf_basis, translations, node_target, out_basis)

    return jax.shard_map(
        per_device, mesh=mesh, in_specs=in_specs, out_specs=out_specs, check_vma=False
    )
```

```python
import jax
import jax.numpy as jnp
from jax import lax
from jax.experimental import pallas as pl
from jax.experimental.pallas import tpu as pltpu
from jax.sharding import PartitionSpec as P

AXES = ("bfly", "rhs")
BF16 = jnp.bfloat16
TILE = 16
VMEM_LIMIT = 12 * 2**20


def from_partner(value, axis, distance):
    mask = 2**distance
    pairs = [(source, source ^ mask) for source in range(lax.axis_size(axis))]
    return lax.ppermute(value, axis, pairs)


def combine(current, partner_part, matrices):
    width = current.shape[1]
    own_term = jnp.einsum(
        "bij,bjc->bic", matrices[:, :, :width], current, preferred_element_type=jnp.float32
    )
    other_term = jnp.einsum(
        "bij,bjc->bic", matrices[:, :, width:], partner_part, preferred_element_type=jnp.float32
    )
    return (own_term + other_term).astype(BF16)


def pack_slots(flat_coefficients, slot_key, capacity, slot_total, target_spot):
    box_count = flat_coefficients.shape[0]
    box_iota = jnp.arange(box_count, dtype=jnp.int32)
    earlier = (slot_key[:, None] == slot_key[None, :]) & (box_iota[None, :] < box_iota[:, None])
    order_within = jnp.sum(earlier.astype(jnp.int32), axis=1)
    slot_of_box = slot_key * capacity + order_within
    selector = jnp.arange(slot_total, dtype=jnp.int32)[:, None] == slot_of_box[None, :]
    outgoing = jnp.dot(
        selector.astype(BF16), flat_coefficients, preferred_element_type=jnp.float32
    ).astype(BF16)
    outgoing_spot = jnp.sum(jnp.where(selector, target_spot[None, :] + 1, 0), axis=1) - 1
    return (outgoing, outgoing_spot)


def exchange_every_level(right_sides, leaf_basis, translations, node_target, out_basis):
    box_count = leaf_basis.shape[0]
    rank_width = leaf_basis.shape[1]
    leaf_rows = leaf_basis.shape[2]
    column_count = right_sides.shape[1]
    point_rows = right_sides.reshape(box_count, leaf_rows, column_count)
    coefficients = jnp.einsum(
        "brl,blc->brc", leaf_basis, point_rows, preferred_element_type=jnp.float32
    ).astype(BF16)
    local_levels = box_count.bit_length() - 1
    for level_index in range(local_levels):
        span = 2**level_index
        blocks = coefficients.reshape(box_count // (2 * span), 2, span, rank_width, column_count)
        partner_part = jnp.flip(blocks, 1).reshape(box_count, rank_width, column_count)
        coefficients = combine(coefficients, partner_part, translations[:, level_index])
    device_count = lax.axis_size(AXES)
    device_levels = device_count.bit_length() - 1
    for section_index in range(device_levels):
        partner_part = from_partner(coefficients, AXES, section_index)
        coefficients = combine(
            coefficients, partner_part, translations[:, local_levels + section_index]
        )
    target_device = node_target // box_count
    target_spot = node_target % box_count
    box_iota = jnp.arange(box_count, dtype=jnp.int32)
    flat_coefficients = coefficients.reshape(box_count, rank_width * column_count)
    capacity = max(1, box_count // device_count)
    slot_total = device_count * capacity
    outgoing, outgoing_spot = pack_slots(
        flat_coefficients, target_device, capacity, slot_total, target_spot
    )
    incoming, incoming_spot = (
        lax.all_to_all(outgoing, AXES, split_axis=0, concat_axis=0, tiled=True),
        lax.all_to_all(outgoing_spot, AXES, split_axis=0, concat_axis=0, tiled=True),
    )
    placement_table = (box_iota[:, None] == incoming_spot[None, :]).astype(BF16)
    placed = jnp.dot(placement_table, incoming, preferred_element_type=jnp.float32).astype(BF16)
    placed = placed.reshape(box_count, rank_width, column_count)
    applied = jnp.einsum("brl,brc->blc", out_basis, placed, preferred_element_type=jnp.float32)
    return applied.astype(BF16).reshape(box_count * leaf_rows, column_count)


def product(matrix, rows):
    return jnp.dot(matrix, rows, preferred_element_type=jnp.float32).astype(BF16)


def stacked(first, second):
    return jnp.concatenate([first, second], axis=0)


def products(first, second, own, other):
    width = own.shape[0]
    turned = jnp.concatenate([second[:, width:], second[:, :width]], axis=1)
    both = product(stacked(first, turned), stacked(own, other))
    return both[:width], both[width:]


def own_half():
    return lax.axis_index("bfly") // 4


def own_place():
    return lax.axis_index("bfly") % 4


def first_box(place):
    return (place % 2) * 4 + (place // 2) * 2


def level_rows(trans_ref, rank, i4, place, i0, level, count):
    return trans_ref.at[i4, :, place % 2, place // 2, i0, pl.ds(level * rank, count * rank)]


def start_all(pairs, sem):
    copies = [pltpu.make_async_copy(source, target, sem) for source, target in pairs]
    for copy in copies:
        copy.start()
    return copies


BOTH = pl.ds(0, 2)


def last_level(rank, trans_ref, i4, r, side, rows_ref):
    slots = rows_ref.reshape(2, rank, trans_ref.shape[-1])
    return level_rows(trans_ref, rank, i4, own_place() ^ r, own_half() ^ side, 8, 1), slots


def spot_tile(target, boxes, columns):
    row = lax.broadcasted_iota(jnp.int32, (TILE, columns), 0)
    tile = target[boxes[-1]] % 32
    for index, box in enumerate(boxes[:-1]):
        tile = jnp.where(row == index, target[box] % 32, tile)
    return tile.astype(jnp.float32).astype(BF16)


def late_tile(target, i4, r, columns):
    base = i4 * 16 + first_box(own_place() ^ r) + 1 - own_half()
    return spot_tile(target, (base, base + 8), columns)


def pack_kernel(rank, target_ref, trans_ref, *refs):
    out_refs, (target, sem, target_sem) = refs[:3], refs[3:]
    group, columns = lax.axis_index("groups"), trans_ref.shape[-1]
    target_copy = pltpu.make_async_copy(target_ref, target, target_sem)
    target_copy.start()
    pairs = []
    for r in (3, 2, 1):
        ref = out_refs[r - 1]
        slots = ref.at[pl.ds(0, 8 * rank)].reshape(2, 2, 2 * rank, columns)
        pairs.append((level_rows(trans_ref, rank, group, own_place() ^ r, BOTH, 6, 2), slots))
        pairs.append(last_level(rank, trans_ref, group, r, 1, ref.at[pl.ds(8 * rank, 2 * rank)]))
    copies = start_all(pairs, sem)
    target_copy.wait()
    for r in (3, 2, 1):
        out_refs[r - 1][pl.ds(10 * rank, TILE), :] = late_tile(target, group, r, columns)
    for copy in copies:
        copy.wait()


def gather_kernel(rank, near1, near2, near3, out_ref):
    for index, ref in enumerate((near1, near2, near3)):
        out_ref[index] = ref[pl.ds(0, 8 * rank), :]


def late_kernel(rank, late_ref, near1, near2, near3, out_ref):
    tile = []
    for r, (ref, at) in enumerate(((late_ref, 0), (near1, 8), (near2, 8), (near3, 8))):
        out_ref[pl.ds(2 * r * rank, 2 * rank), :] = ref[pl.ds(at * rank, 2 * rank), :]
        tile.append(ref[pl.ds((at + 2) * rank, TILE), :].astype(jnp.float32)[0:2])
    pad = jnp.zeros((TILE - 8, out_ref.shape[-1]), jnp.float32)
    out_ref[pl.ds(8 * rank, TILE), :] = jnp.concatenate([*tile, pad], axis=0).astype(BF16)


def local_kernel(
    levels, rs_ref, leaf_ref, trans_ref, grid_ref, target_ref, out_ref, next_ref, pair_ref, stay0, stay1, stay2, stay3, late_ref,
    rs, leaf, trans, ping, pong, target_smem, sem, trans_sem, rest_sem, target_sem
):
    rank = leaf_ref.shape[1]
    target_copy = pltpu.make_async_copy(target_ref, target_smem, target_sem)
    target_copy.start()
    boxes = leaf_ref.shape[0]
    step = boxes // 4
    loads = []
    for part in range(4):
        rows = pl.ds(part * step, step)
        loads.append(
            (
                pltpu.make_async_copy(rs_ref.at[rows], rs.at[rows], sem.at[part, 0]),
                pltpu.make_async_copy(leaf_ref.at[rows], leaf.at[rows], sem.at[part, 1]),
            )
        )
    level_loads = [
        pltpu.make_async_copy(trans_ref.at[:, level], trans.at[level], trans_sem.at[level])
        for level in range(levels)
    ]
    level_loads.append(
        pltpu.make_async_copy(trans_ref.at[:, levels], next_ref, trans_sem.at[levels])
    )
    for pair in loads:
        for copy in pair:
            copy.start()
    for copy in level_loads:
        copy.start()
    group, columns = lax.axis_index("groups"), grid_ref.shape[-1]
    rest = [(level_rows(grid_ref, rank, BOTH, own_place(), BOTH, 6, 2), pair_ref)]
    two = pl.ds(0, 2 * rank)
    stay_refs = (stay0, stay1, stay2, stay3)
    for r, ref in enumerate(stay_refs):
        for i4 in range(2):
            rows = ref.at[pl.ds(2 * i4 * rank, 2 * rank)]
            rest.append(last_level(rank, grid_ref, i4, r, 0, rows))
    rest.append(last_level(rank, grid_ref, group, 0, 1, late_ref.at[two]))
    rest = start_all(rest, rest_sem)
    target_copy.wait()
    for r, ref in enumerate(stay_refs):
        base = first_box(own_place() ^ r) + own_half()
        spots = [base + q * 8 for q in range(4)]
        ref[pl.ds(4 * rank, TILE), :] = spot_tile(target_smem, spots, columns)
    late_ref[pl.ds(2 * rank, TILE), :] = late_tile(target_smem, group, 0, columns)
    for part in range(4):
        for copy in loads[part]:
            copy.wait()
        for box in range(part * step, (part + 1) * step):
            ping[box] = product(leaf[box], rs[box])
    source, target = ping, pong
    for level in range(levels):
        level_loads[level].wait()
        if level == levels - 1:
            target = out_ref
        for box in range(boxes):
            rows = stacked(source[box], source[box ^ (1 << level)])
            target[box] = product(trans[level, box], rows)
        source, target = target, source
    level_loads[levels].wait()
    for copy in rest:
        copy.wait()


def chip_kernel(own_ref, other_ref, trans_ref, *out_refs):
    own = own_place()
    for r in (1, 2, 3, 0):
        base = first_box(own ^ r)
        for q in range(4):
            for i0 in range(2):
                box = base + q * 8 + i0
                rows = stacked(own_ref[box], other_ref[box])
                out_refs[r][q, i0] = product(trans_ref[box], rows)


def quad_kernel(
    rank, box0, box1, box2, box3, pair_ref, near1, near2, near3, far_ref, keep_ref, send_ref, middle
):
    boxes = (box0, box1, box2, box3)
    half, group = own_half(), lax.axis_index("groups")

    def matrix(r, h, i3, i0, level):
        if r == 0:
            return pair_ref[group ^ h, i3, i0, pl.ds(level * rank, rank)]
        ref = far_ref.at[r - 1] if h else (near1, near2, near3)[r - 1]
        start = pl.multiple_of(((i3 * 2 + i0) * 2 + level) * rank, TILE)
        return ref[pl.ds(start, rank), :]

    slots = [(h, i3) for h in range(2) for i3 in range(2)]
    for r in (0, 2):
        for h, i3 in slots:
            q = (group ^ h) * 2 + i3
            for i0 in range(2):
                pair = matrix(r, h, i3, i0, 0), matrix(r + 1, h, i3, i0, 0)
                both = products(*pair, boxes[r][q, i0], boxes[r + 1][q, i0])
                middle[r, q, i0], middle[r + 1, q, i0] = both
    for out_ref, bit in ((send_ref, 1 - half), (keep_ref, half)):
        for r in (0, 1):
            for h, i3 in slots:
                q = (group ^ h) * 2 + i3
                pair = matrix(r, h, i3, bit, 1), matrix(r + 2, h, i3, bit, 1)
                both = products(*pair, middle[r, q, bit], middle[r + 2, q, bit])
                out_ref[r, q], out_ref[r + 2, q] = both


def last_matrices(rank, bit, stay0, stay1, stay2, stay3, here_ref, cross_ref):
    group = lax.axis_index("groups")

    def source(side, r, h):
        if side:
            return (here_ref, cross_ref)[h], 2 * r, 8 * rank, 2 * r, 2 * r
        i4 = group ^ h
        return (stay0, stay1, stay2, stay3)[r], 2 * i4, 4 * rank, i4, None

    boxes = []
    for side in range(2):
        for r in range(4):
            for h in range(2):
                ref, first, tile, i4, row = source(side, r, h)
                spots = ref[pl.ds(tile, TILE), :].astype(jnp.float32)
                spots = jnp.where(i4 == 0, spots[0:2], spots[2:4]) if row is None else spots[row : row + 2]
                matrix = ref[pl.ds(pl.multiple_of((first + bit) * rank, TILE), rank), :]
                boxes.append((side, r, h, matrix, jnp.where(bit == 0, spots[0:1], spots[1:2])))
    return boxes


def both_halves(side, r, q, keep_ref, recv_ref):
    sides = (keep_ref[r, q], recv_ref[r, q])
    return stacked(sides[side], sides[1 - side])


def send_kernel(rank, keep_ref, recv_ref, *refs):
    group, bit = lax.axis_index("groups"), 1 - lax.axis_index("rhs")
    out_ref, tile = refs[-1], []
    for index, (side, r, h, matrix, spot) in enumerate(last_matrices(rank, bit, *refs[:-1])):
        rows = both_halves(side, r, (group ^ h) * 2 + bit, keep_ref, recv_ref)
        out_ref[pl.ds(index * rank, rank), :] = product(matrix, rows)
        tile.append(spot)
    out_ref[pl.ds(16 * rank, TILE), :] = jnp.concatenate(tile, axis=0).astype(BF16)


def write_rows(box, spot, slot, basis_ref, result, out_ref, sem):
    result[slot] = lax.dot_general(
        basis_ref[spot], box, (((0,), (0,)), ((), ())), preferred_element_type=jnp.float32
    ).astype(BF16)
    copy = pltpu.make_async_copy(result.at[slot], out_ref.at[spot], sem)
    copy.start()
    return copy


def own_kernel(rank, keep_ref, recv_ref, *refs):
    *matrix_refs, basis_ref, out_ref, result, sem, final = refs
    group, bit = lax.axis_index("groups"), lax.axis_index("rhs")
    copies = []
    boxes = last_matrices(rank, bit, *matrix_refs)
    spots = [jnp.max(spot).astype(jnp.int32) for *_, spot in boxes]
    for slot, (side, r, h, matrix, _) in enumerate(boxes):
        rows = both_halves(side, r, (group ^ h) * 2 + bit, keep_ref, recv_ref)
        final[slot] = product(matrix, rows)
    for slot, spot in enumerate(spots):
        copies.append(write_rows(final[slot], spot, slot, basis_ref, result, out_ref, sem))
    for copy in copies:
        copy.wait()


def output_kernel(rank, box_ref, basis_ref, *refs):
    out_ref, result, sem = refs[-3:]
    tile = box_ref[pl.ds(16 * rank, TILE), :].astype(jnp.float32)
    spots = [jnp.max(tile[slot : slot + 1]).astype(jnp.int32) for slot in range(16)]
    copies = []
    for slot in range(16):
        box = box_ref[pl.ds(slot * rank, rank), :]
        copies.append(write_rows(box, spots[slot], slot, basis_ref, result, out_ref, sem))
    for copy in copies:
        copy.wait()


def call(kernel, out_shapes, in_spaces, out_spaces, scratch, flops, moved, aliases=None):
    run = pl.pallas_call(
        kernel,
        out_shape=out_shapes,
        in_specs=[pl.BlockSpec(memory_space=space) for space in in_spaces],
        out_specs=jax.tree.map(lambda space: pl.BlockSpec(memory_space=space), out_spaces),
        scratch_shapes=scratch,
        input_output_aliases=aliases or {},
        compiler_params=pltpu.CompilerParams(vmem_limit_bytes=VMEM_LIMIT),
        cost_estimate=pl.CostEstimate(flops=flops, bytes_accessed=moved, transcendentals=0),
    )

    def placed(*operands):
        return run(
            *(
                pltpu.with_memory_space_constraint(operand, space) if space == pltpu.HBM else operand
                for operand, space in zip(operands, in_spaces)
            )
        )

    return placed


def shape(*dims):
    return jax.ShapeDtypeStruct(dims, BF16)


def bind(kernel, *values):
    return lambda *refs: kernel(*values, *refs)


def move_early(right_sides, leaf_basis, translations, node_target, out_basis):
    boxes, rank, leaf_rows = leaf_basis.shape
    columns = right_sides.shape[1]
    local_levels = boxes.bit_length() - 1
    width = 2 * rank
    block = 2 * rank * columns * 2
    hbm, vmem, smem, dma = pltpu.HBM, pltpu.VMEM, pltpu.SMEM, pltpu.SemaphoreType.DMA
    def across(value, mask):
        return lax.ppermute(value, AXES, [(s, s ^ mask) for s in range(16)])

    def swapped(value):
        return lax.ppermute(value, "groups", [(0, 1), (1, 0)])

    grid = translations.reshape(2, 2, 2, 2, 2, -1, width)
    part = shape(2 * rank + TILE, width)
    near_part = shape(10 * rank + TILE, width)
    stay_part = shape(4 * rank + TILE, width)
    near = call(
        bind(pack_kernel, rank),
        (near_part,) * 3,
        (hbm, hbm),
        (vmem,) * 3,
        [smem((boxes,), jnp.int32), dma, dma],
        0,
        2**20,
    )(node_target, grid)
    right_sides, near = lax.optimization_barrier((right_sides, near))
    near = [across(near[r - 1], 2 * r) for r in (1, 2, 3)]
    coefficients, chip_translations, own_pair, *stay, late = call(
        bind(local_kernel, local_levels),
        (
            shape(boxes, rank, columns),
            shape(boxes, rank, width),
            shape(2, 2, 2, 2 * rank, width),
        )
        + (stay_part,) * 4
        + (part,),
        (hbm,) * 5,
        (vmem,) * 8,
        [
            vmem((boxes, leaf_rows, columns), BF16),
            vmem((boxes, rank, leaf_rows), BF16),
            vmem((local_levels, boxes, rank, width), BF16),
            vmem((boxes, rank, columns), BF16),
            vmem((boxes, rank, columns), BF16),
            smem((boxes,), jnp.int32),
            dma((4, 2)),
            dma((local_levels + 1,)),
            dma,
            dma,
        ],
        boxes * rank * columns * 2 * (leaf_rows + local_levels * width),
        6 * 2**20,
    )(
        right_sides.reshape(boxes, leaf_rows, columns), leaf_basis, translations, grid, node_target
    )
    coefficients, near = lax.optimization_barrier((coefficients, near))
    partner = across(coefficients, 1)
    far = call(bind(gather_kernel, rank), shape(3, 8 * rank, width), (vmem,) * 3, vmem, [], 0, 2**20)(*near)
    far = swapped(far)
    slots = call(
        chip_kernel,
        (shape(4, 2, rank, columns),) * 4,
        (vmem,) * 3,
        (vmem,) * 4,
        [],
        boxes * block * width,
        2**21,
    )(coefficients, partner, chip_translations)
    slots = [slots[0]] + [across(slots[r], 2 * r) for r in (1, 2, 3)]
    _, late = lax.optimization_barrier((slots[1], late))
    here = call(
        bind(late_kernel, rank), shape(8 * rank + TILE, width), (vmem,) * 4, vmem, [], 0, 2**20
    )(late, *near)
    here = across(here, 8)
    keep, send = call(
        bind(quad_kernel, rank),
        (shape(4, 4, rank, columns), shape(4, 4, rank, columns)),
        (vmem,) * 9,
        (vmem,) * 2,
        [vmem((4, 4, 2, rank, columns), BF16)],
        2 * boxes * block * width,
        2**21,
    )(*slots, own_pair, *near, far)
    received = across(send, 8)
    stay, _ = lax.optimization_barrier((stay, send))
    stay = [stay[0]] + [across(stay[r], 2 * r) for r in (1, 2, 3)]
    here, stay[1], stay[2], stay[3] = lax.optimization_barrier((here, stay[1], stay[2], stay[3]))
    cross = swapped(here)
    basis = out_basis
    matrices = (*stay, here, cross)
    send = call(
        bind(send_kernel, rank),
        shape(16 * rank + TILE, columns),
        (vmem,) * 8,
        vmem,
        [],
        boxes * block * width // 2,
        2**20,
    )(keep, received, *matrices)
    partner = across(send, 1)
    rows = shape(boxes, leaf_rows, columns)
    scratch = [vmem((16, leaf_rows, columns), BF16), dma]
    applied = call(
        bind(own_kernel, rank),
        rows,
        (vmem,) * 9,
        hbm,
        [*scratch, vmem((16, rank, columns), BF16)],
        boxes * block * width,
        2**21,
    )(keep, received, *matrices, basis)
    applied = call(
        bind(output_kernel, rank),
        rows,
        (vmem, vmem, hbm),
        hbm,
        scratch,
        boxes * block * width,
        2**21,
        {2: 0},
    )(partner, basis, applied)
    return applied.reshape(boxes * leaf_rows, columns)


def solution(mesh):
    in_specs = (
        P(("groups", "bfly", "rhs"), None),
        P(("bfly", "rhs"), None, None),
        P(("bfly", "rhs"), None, None, None),
        P(("bfly", "rhs")),
        P(("bfly", "rhs"), None, None),
    )
    out_specs = P(("groups", "bfly", "rhs"), None)

    def per_device(right_sides, leaf_basis, translations, node_target, out_basis):
        devices = lax.axis_size(AXES)
        fits = devices == 16 and lax.axis_size("groups") == 2 and leaf_basis.shape[0] == 32
        apply = move_early if fits else exchange_every_level
        return apply(right_sides, leaf_basis, translations, node_target, out_basis)

    return jax.shard_map(
        per_device, mesh=mesh, in_specs=in_specs, out_specs=out_specs, check_vma=False
    )
```

```python
import jax
import jax.numpy as jnp
from jax import lax
from jax.experimental import pallas as pl
from jax.experimental.pallas import tpu as pltpu
from jax.sharding import PartitionSpec as P

AXES = ("bfly", "rhs")
BF16 = jnp.bfloat16
TILE = 16
VMEM_LIMIT = 12 * 2**20


def from_partner(value, axis, distance):
    mask = 2**distance
    pairs = [(source, source ^ mask) for source in range(lax.axis_size(axis))]
    return lax.ppermute(value, axis, pairs)


def combine(current, partner_part, matrices):
    width = current.shape[1]
    own_term = jnp.einsum(
        "bij,bjc->bic", matrices[:, :, :width], current, preferred_element_type=jnp.float32
    )
    other_term = jnp.einsum(
        "bij,bjc->bic", matrices[:, :, width:], partner_part, preferred_element_type=jnp.float32
    )
    return (own_term + other_term).astype(BF16)


def pack_slots(flat_coefficients, slot_key, capacity, slot_total, target_spot):
    box_count = flat_coefficients.shape[0]
    box_iota = jnp.arange(box_count, dtype=jnp.int32)
    earlier = (slot_key[:, None] == slot_key[None, :]) & (box_iota[None, :] < box_iota[:, None])
    order_within = jnp.sum(earlier.astype(jnp.int32), axis=1)
    slot_of_box = slot_key * capacity + order_within
    selector = jnp.arange(slot_total, dtype=jnp.int32)[:, None] == slot_of_box[None, :]
    outgoing = jnp.dot(
        selector.astype(BF16), flat_coefficients, preferred_element_type=jnp.float32
    ).astype(BF16)
    outgoing_spot = jnp.sum(jnp.where(selector, target_spot[None, :] + 1, 0), axis=1) - 1
    return (outgoing, outgoing_spot)


def exchange_every_level(right_sides, leaf_basis, translations, node_target, out_basis):
    box_count = leaf_basis.shape[0]
    rank_width = leaf_basis.shape[1]
    leaf_rows = leaf_basis.shape[2]
    column_count = right_sides.shape[1]
    point_rows = right_sides.reshape(box_count, leaf_rows, column_count)
    coefficients = jnp.einsum(
        "brl,blc->brc", leaf_basis, point_rows, preferred_element_type=jnp.float32
    ).astype(BF16)
    local_levels = box_count.bit_length() - 1
    for level_index in range(local_levels):
        span = 2**level_index
        blocks = coefficients.reshape(box_count // (2 * span), 2, span, rank_width, column_count)
        partner_part = jnp.flip(blocks, 1).reshape(box_count, rank_width, column_count)
        coefficients = combine(coefficients, partner_part, translations[:, level_index])
    device_count = lax.axis_size(AXES)
    device_levels = device_count.bit_length() - 1
    for section_index in range(device_levels):
        partner_part = from_partner(coefficients, AXES, section_index)
        coefficients = combine(
            coefficients, partner_part, translations[:, local_levels + section_index]
        )
    target_device = node_target // box_count
    target_spot = node_target % box_count
    box_iota = jnp.arange(box_count, dtype=jnp.int32)
    flat_coefficients = coefficients.reshape(box_count, rank_width * column_count)
    capacity = max(1, box_count // device_count)
    slot_total = device_count * capacity
    outgoing, outgoing_spot = pack_slots(
        flat_coefficients, target_device, capacity, slot_total, target_spot
    )
    incoming, incoming_spot = (
        lax.all_to_all(outgoing, AXES, split_axis=0, concat_axis=0, tiled=True),
        lax.all_to_all(outgoing_spot, AXES, split_axis=0, concat_axis=0, tiled=True),
    )
    placement_table = (box_iota[:, None] == incoming_spot[None, :]).astype(BF16)
    placed = jnp.dot(placement_table, incoming, preferred_element_type=jnp.float32).astype(BF16)
    placed = placed.reshape(box_count, rank_width, column_count)
    applied = jnp.einsum("brl,brc->blc", out_basis, placed, preferred_element_type=jnp.float32)
    return applied.astype(BF16).reshape(box_count * leaf_rows, column_count)


def product(matrix, rows):
    return jnp.dot(matrix, rows, preferred_element_type=jnp.float32).astype(BF16)


def stacked(first, second):
    return jnp.concatenate([first, second], axis=0)


def products(first, second, own, other):
    width = own.shape[0]
    turned = jnp.concatenate([second[:, width:], second[:, :width]], axis=1)
    both = product(stacked(first, turned), stacked(own, other))
    return both[:width], both[width:]


def own_half():
    return lax.axis_index("bfly") // 4


def own_place():
    return lax.axis_index("bfly") % 4


def first_box(place):
    return (place % 2) * 4 + (place // 2) * 2


def level_rows(trans_ref, rank, i4, place, i0, level, count):
    return trans_ref.at[i4, :, place % 2, place // 2, i0, pl.ds(level * rank, count * rank)]


def start_all(pairs, sem):
    copies = [pltpu.make_async_copy(source, target, sem) for source, target in pairs]
    for copy in copies:
        copy.start()
    return copies


BOTH = pl.ds(0, 2)


def last_level(rank, trans_ref, i4, r, side, rows_ref):
    slots = rows_ref.reshape(2, rank, trans_ref.shape[-1])
    return level_rows(trans_ref, rank, i4, own_place() ^ r, own_half() ^ side, 8, 1), slots


def spot_tile(target, boxes, columns):
    row = lax.broadcasted_iota(jnp.int32, (TILE, columns), 0)
    tile = target[boxes[-1]] % 32
    for index, box in enumerate(boxes[:-1]):
        tile = jnp.where(row == index, target[box] % 32, tile)
    return tile.astype(jnp.float32).astype(BF16)


def late_tile(target, i4, r, columns):
    base = i4 * 16 + first_box(own_place() ^ r) + 1 - own_half()
    return spot_tile(target, (base, base + 8), columns)


def pack_kernel(rank, target_ref, trans_ref, *refs):
    out_refs, (target, sem, target_sem) = refs[:3], refs[3:]
    group, columns = lax.axis_index("groups"), trans_ref.shape[-1]
    target_copy = pltpu.make_async_copy(target_ref, target, target_sem)
    target_copy.start()
    pairs = []
    for r in (3, 2, 1):
        ref = out_refs[r - 1]
        slots = ref.at[pl.ds(0, 8 * rank)].reshape(2, 2, 2 * rank, columns)
        pairs.append((level_rows(trans_ref, rank, group, own_place() ^ r, BOTH, 6, 2), slots))
        pairs.append(last_level(rank, trans_ref, group, r, 1, ref.at[pl.ds(8 * rank, 2 * rank)]))
    copies = start_all(pairs, sem)
    target_copy.wait()
    for r in (3, 2, 1):
        out_refs[r - 1][pl.ds(10 * rank, TILE), :] = late_tile(target, group, r, columns)
    for copy in copies:
        copy.wait()


def gather_kernel(rank, near1, near2, near3, out_ref):
    for index, ref in enumerate((near1, near2, near3)):
        out_ref[index] = ref[pl.ds(0, 8 * rank), :]


def late_kernel(rank, late_ref, near1, near2, near3, out_ref):
    tile = []
    for r, (ref, at) in enumerate(((late_ref, 0), (near1, 8), (near2, 8), (near3, 8))):
        out_ref[pl.ds(2 * r * rank, 2 * rank), :] = ref[pl.ds(at * rank, 2 * rank), :]
        tile.append(ref[pl.ds((at + 2) * rank, TILE), :].astype(jnp.float32)[0:2])
    pad = jnp.zeros((TILE - 8, out_ref.shape[-1]), jnp.float32)
    out_ref[pl.ds(8 * rank, TILE), :] = jnp.concatenate([*tile, pad], axis=0).astype(BF16)


def local_kernel(
    levels, rs_ref, leaf_ref, trans_ref, grid_ref, target_ref, out_ref, next_ref, pair_ref, stay0, stay1, stay2, stay3, late_ref,
    rs, leaf, trans, ping, pong, target_smem, sem, trans_sem, rest_sem, target_sem
):
    rank = leaf_ref.shape[1]
    target_copy = pltpu.make_async_copy(target_ref, target_smem, target_sem)
    target_copy.start()
    boxes = leaf_ref.shape[0]
    step = boxes // 4
    loads = []
    for part in range(4):
        rows = pl.ds(part * step, step)
        loads.append(
            (
                pltpu.make_async_copy(rs_ref.at[rows], rs.at[rows], sem.at[part, 0]),
                pltpu.make_async_copy(leaf_ref.at[rows], leaf.at[rows], sem.at[part, 1]),
            )
        )
    level_loads = [
        pltpu.make_async_copy(trans_ref.at[:, level], trans.at[level], trans_sem.at[level])
        for level in range(levels)
    ]
    level_loads.append(
        pltpu.make_async_copy(trans_ref.at[:, levels], next_ref, trans_sem.at[levels])
    )
    for pair in loads:
        for copy in pair:
            copy.start()
    for copy in level_loads:
        copy.start()
    group, columns = lax.axis_index("groups"), grid_ref.shape[-1]
    rest = [(level_rows(grid_ref, rank, BOTH, own_place(), BOTH, 6, 2), pair_ref)]
    two = pl.ds(0, 2 * rank)
    stay_refs = (stay0, stay1, stay2, stay3)
    for r, ref in enumerate(stay_refs):
        for i4 in range(2):
            rows = ref.at[pl.ds(2 * i4 * rank, 2 * rank)]
            rest.append(last_level(rank, grid_ref, i4, r, 0, rows))
    rest.append(last_level(rank, grid_ref, group, 0, 1, late_ref.at[two]))
    rest = start_all(rest, rest_sem)
    target_copy.wait()
    for r, ref in enumerate(stay_refs):
        base = first_box(own_place() ^ r) + own_half()
        spots = [base + q * 8 for q in range(4)]
        ref[pl.ds(4 * rank, TILE), :] = spot_tile(target_smem, spots, columns)
    late_ref[pl.ds(2 * rank, TILE), :] = late_tile(target_smem, group, 0, columns)
    for part in range(4):
        for copy in loads[part]:
            copy.wait()
        for box in range(part * step, (part + 1) * step):
            ping[box] = product(leaf[box], rs[box])
    source, target = ping, pong
    for level in range(levels):
        level_loads[level].wait()
        if level == levels - 1:
            target = out_ref
        for box in range(boxes):
            rows = stacked(source[box], source[box ^ (1 << level)])
            target[box] = product(trans[level, box], rows)
        source, target = target, source
    level_loads[levels].wait()
    for copy in rest:
        copy.wait()


def chip_kernel(own_ref, other_ref, trans_ref, *out_refs):
    own = own_place()
    for r in (1, 2, 3, 0):
        base = first_box(own ^ r)
        for q in range(4):
            for i0 in range(2):
                box = base + q * 8 + i0
                rows = stacked(own_ref[box], other_ref[box])
                out_refs[r][q, i0] = product(trans_ref[box], rows)


def quad_kernel(
    rank, box0, box1, box2, box3, pair_ref, near1, near2, near3, far_ref, keep_ref, send_ref, middle
):
    boxes = (box0, box1, box2, box3)
    half, group = own_half(), lax.axis_index("groups")

    def matrix(r, h, i3, i0, level):
        if r == 0:
            return pair_ref[group ^ h, i3, i0, pl.ds(level * rank, rank)]
        ref = far_ref.at[r - 1] if h else (near1, near2, near3)[r - 1]
        start = pl.multiple_of(((i3 * 2 + i0) * 2 + level) * rank, TILE)
        return ref[pl.ds(start, rank), :]

    slots = [(h, i3) for h in range(2) for i3 in range(2)]
    for r in (0, 2):
        for h, i3 in slots:
            q = (group ^ h) * 2 + i3
            for i0 in range(2):
                pair = matrix(r, h, i3, i0, 0), matrix(r + 1, h, i3, i0, 0)
                both = products(*pair, boxes[r][q, i0], boxes[r + 1][q, i0])
                middle[r, q, i0], middle[r + 1, q, i0] = both
    for out_ref, bit in ((send_ref, 1 - half), (keep_ref, half)):
        for r in (0, 1):
            for h, i3 in slots:
                q = (group ^ h) * 2 + i3
                pair = matrix(r, h, i3, bit, 1), matrix(r + 2, h, i3, bit, 1)
                both = products(*pair, middle[r, q, bit], middle[r + 2, q, bit])
                out_ref[r, q], out_ref[r + 2, q] = both


def last_matrices(rank, bit, stay0, stay1, stay2, stay3, here_ref, cross_ref):
    group = lax.axis_index("groups")

    def source(side, r, h):
        if side:
            return (here_ref, cross_ref)[h], 2 * r, 8 * rank, 2 * r, 2 * r
        i4 = group ^ h
        return (stay0, stay1, stay2, stay3)[r], 2 * i4, 4 * rank, i4, None

    boxes = []
    for side in range(2):
        for r in range(4):
            for h in range(2):
                ref, first, tile, i4, row = source(side, r, h)
                spots = ref[pl.ds(tile, TILE), :].astype(jnp.float32)
                spots = jnp.where(i4 == 0, spots[0:2], spots[2:4]) if row is None else spots[row : row + 2]
                matrix = ref[pl.ds(pl.multiple_of((first + bit) * rank, TILE), rank), :]
                boxes.append((side, r, h, matrix, jnp.where(bit == 0, spots[0:1], spots[1:2])))
    return boxes


def both_halves(side, r, q, keep_ref, recv_ref):
    sides = (keep_ref[r, q], recv_ref[r, q])
    return stacked(sides[side], sides[1 - side])


def send_kernel(rank, keep_ref, recv_ref, *refs):
    group, bit = lax.axis_index("groups"), 1 - lax.axis_index("rhs")
    out_ref, tile = refs[-1], []
    for index, (side, r, h, matrix, spot) in enumerate(last_matrices(rank, bit, *refs[:-1])):
        rows = both_halves(side, r, (group ^ h) * 2 + bit, keep_ref, recv_ref)
        out_ref[pl.ds(index * rank, rank), :] = product(matrix, rows)
        tile.append(spot)
    out_ref[pl.ds(16 * rank, TILE), :] = jnp.concatenate(tile, axis=0).astype(BF16)


def write_rows(box, spot, slot, basis_ref, result, out_ref, sem):
    result[slot] = lax.dot_general(
        basis_ref[spot], box, (((0,), (0,)), ((), ())), preferred_element_type=jnp.float32
    ).astype(BF16)
    copy = pltpu.make_async_copy(result.at[slot], out_ref.at[spot], sem)
    copy.start()
    return copy


def own_kernel(rank, keep_ref, recv_ref, *refs):
    *matrix_refs, basis_ref, out_ref, result, sem, final = refs
    group, bit = lax.axis_index("groups"), lax.axis_index("rhs")
    copies = []
    boxes = last_matrices(rank, bit, *matrix_refs)
    spots = [jnp.max(spot).astype(jnp.int32) for *_, spot in boxes]
    for slot, (side, r, h, matrix, _) in enumerate(boxes):
        rows = both_halves(side, r, (group ^ h) * 2 + bit, keep_ref, recv_ref)
        final[slot] = product(matrix, rows)
    for slot, spot in enumerate(spots):
        copies.append(write_rows(final[slot], spot, slot, basis_ref, result, out_ref, sem))
    for copy in copies:
        copy.wait()


def output_kernel(rank, box_ref, basis_ref, *refs):
    out_ref, result, sem = refs[-3:]
    tile = box_ref[pl.ds(16 * rank, TILE), :].astype(jnp.float32)
    spots = [jnp.max(tile[slot : slot + 1]).astype(jnp.int32) for slot in range(16)]
    copies = []
    for slot in range(16):
        box = box_ref[pl.ds(slot * rank, rank), :]
        copies.append(write_rows(box, spots[slot], slot, basis_ref, result, out_ref, sem))
    for copy in copies:
        copy.wait()


def call(kernel, out_shapes, in_spaces, out_spaces, scratch, flops, moved, aliases=None):
    run = pl.pallas_call(
        kernel,
        out_shape=out_shapes,
        in_specs=[pl.BlockSpec(memory_space=space) for space in in_spaces],
        out_specs=jax.tree.map(lambda space: pl.BlockSpec(memory_space=space), out_spaces),
        scratch_shapes=scratch,
        input_output_aliases=aliases or {},
        compiler_params=pltpu.CompilerParams(vmem_limit_bytes=VMEM_LIMIT),
        cost_estimate=pl.CostEstimate(flops=flops, bytes_accessed=moved, transcendentals=0),
    )

    def placed(*operands):
        return run(
            *(
                pltpu.with_memory_space_constraint(operand, space) if space == pltpu.HBM else operand
                for operand, space in zip(operands, in_spaces)
            )
        )

    return placed


def shape(*dims):
    return jax.ShapeDtypeStruct(dims, BF16)


def bind(kernel, *values):
    return lambda *refs: kernel(*values, *refs)


def move_early(right_sides, leaf_basis, translations, node_target, out_basis):
    boxes, rank, leaf_rows = leaf_basis.shape
    columns = right_sides.shape[1]
    local_levels = boxes.bit_length() - 1
    width = 2 * rank
    block = 2 * rank * columns * 2
    hbm, vmem, smem, dma = pltpu.HBM, pltpu.VMEM, pltpu.SMEM, pltpu.SemaphoreType.DMA
    def across(value, mask):
        return lax.ppermute(value, AXES, [(s, s ^ mask) for s in range(16)])

    def swapped(value):
        return lax.ppermute(value, "groups", [(0, 1), (1, 0)])

    grid = translations.reshape(2, 2, 2, 2, 2, -1, width)
    part = shape(2 * rank + TILE, width)
    near_part = shape(10 * rank + TILE, width)
    stay_part = shape(4 * rank + TILE, width)
    near = call(
        bind(pack_kernel, rank),
        (near_part,) * 3,
        (hbm, hbm),
        (vmem,) * 3,
        [smem((boxes,), jnp.int32), dma, dma],
        0,
        2**20,
    )(node_target, grid)
    right_sides, near = lax.optimization_barrier((right_sides, near))
    near = [across(near[r - 1], 2 * r) for r in (1, 2, 3)]
    coefficients, chip_translations, own_pair, *stay, late = call(
        bind(local_kernel, local_levels),
        (
            shape(boxes, rank, columns),
            shape(boxes, rank, width),
            shape(2, 2, 2, 2 * rank, width),
        )
        + (stay_part,) * 4
        + (part,),
        (hbm,) * 5,
        (vmem,) * 8,
        [
            vmem((boxes, leaf_rows, columns), BF16),
            vmem((boxes, rank, leaf_rows), BF16),
            vmem((local_levels, boxes, rank, width), BF16),
            vmem((boxes, rank, columns), BF16),
            vmem((boxes, rank, columns), BF16),
            smem((boxes,), jnp.int32),
            dma((4, 2)),
            dma((local_levels + 1,)),
            dma,
            dma,
        ],
        boxes * rank * columns * 2 * (leaf_rows + local_levels * width),
        6 * 2**20,
    )(
        right_sides.reshape(boxes, leaf_rows, columns), leaf_basis, translations, grid, node_target
    )
    coefficients, near = lax.optimization_barrier((coefficients, near))
    partner = across(coefficients, 1)
    far = call(bind(gather_kernel, rank), shape(3, 8 * rank, width), (vmem,) * 3, vmem, [], 0, 2**20)(*near)
    far = swapped(far)
    slots = call(
        chip_kernel,
        (shape(4, 2, rank, columns),) * 4,
        (vmem,) * 3,
        (vmem,) * 4,
        [],
        boxes * block * width,
        2**21,
    )(coefficients, partner, chip_translations)
    slots = [slots[0]] + [across(slots[r], 2 * r) for r in (1, 2, 3)]
    _, late = lax.optimization_barrier((slots[1], late))
    here = call(
        bind(late_kernel, rank), shape(8 * rank + TILE, width), (vmem,) * 4, vmem, [], 0, 2**20
    )(late, *near)
    here = across(here, 8)
    keep, send = call(
        bind(quad_kernel, rank),
        (shape(4, 4, rank, columns), shape(4, 4, rank, columns)),
        (vmem,) * 9,
        (vmem,) * 2,
        [vmem((4, 4, 2, rank, columns), BF16)],
        2 * boxes * block * width,
        2**21,
    )(*slots, own_pair, *near, far)
    received = across(send, 8)
    stay, _ = lax.optimization_barrier((stay, send))
    stay = [stay[0]] + [across(stay[r], 2 * r) for r in (1, 2, 3)]
    here, stay[1], stay[3] = lax.optimization_barrier((here, stay[1], stay[3]))
    cross = swapped(here)
    basis = out_basis
    matrices = (*stay, here, cross)
    send = call(
        bind(send_kernel, rank),
        shape(16 * rank + TILE, columns),
        (vmem,) * 8,
        vmem,
        [],
        boxes * block * width // 2,
        2**20,
    )(keep, received, *matrices)
    partner = across(send, 1)
    rows = shape(boxes, leaf_rows, columns)
    scratch = [vmem((16, leaf_rows, columns), BF16), dma]
    applied = call(
        bind(own_kernel, rank),
        rows,
        (vmem,) * 9,
        hbm,
        [*scratch, vmem((16, rank, columns), BF16)],
        boxes * block * width,
        2**21,
    )(keep, received, *matrices, basis)
    applied = call(
        bind(output_kernel, rank),
        rows,
        (vmem, vmem, hbm),
        hbm,
        scratch,
        boxes * block * width,
        2**21,
        {2: 0},
    )(partner, basis, applied)
    return applied.reshape(boxes * leaf_rows, columns)


def solution(mesh):
    in_specs = (
        P(("groups", "bfly", "rhs"), None),
        P(("bfly", "rhs"), None, None),
        P(("bfly", "rhs"), None, None, None),
        P(("bfly", "rhs")),
        P(("bfly", "rhs"), None, None),
    )
    out_specs = P(("groups", "bfly", "rhs"), None)

    def per_device(right_sides, leaf_basis, translations, node_target, out_basis):
        devices = lax.axis_size(AXES)
        fits = devices == 16 and lax.axis_size("groups") == 2 and leaf_basis.shape[0] == 32
        apply = move_early if fits else exchange_every_level
        return apply(right_sides, leaf_basis, translations, node_target, out_basis)

    return jax.shard_map(
        per_device, mesh=mesh, in_specs=in_specs, out_specs=out_specs, check_vma=False
    )
```
